32 devices in a mesh: rows: 8 (over z, x), cols: 4 (over y, core).
Axes of the slice: x: 2, y: 2, z: 4, core: 2. Of those that a mesh axis runs over, the one named last changes fastest.
Arguments:
- tiles: bfloat16 [4096, 4096], P(('rows', 'cols')), may hold values from -0.125 to 0.125
- integral_cd_tile: int32 [4096], P(('rows', 'cols')), may hold values from 0 to 31
- part_dest: int32 [1024, 1], P(('rows', 'cols')), may hold values from 0 to 7; in each aligned block of 32 rows (0 to 31, 32 to 63, ...) at most 8 rows name the same one
- partial_row_place: int32 [1024], P(('rows', 'cols')), may hold values from 0 to 15
- amplitudes: bfloat16 [4, 32, 4096], P('cols', 'rows'), may hold values from -6 to 6
- residual_in: float32 [8, 16, 4096], P('rows', 'cols'), may hold values from -6 to 6
Outputs:
- residual: float32 [8, 16, 4096], P('rows', 'cols')
The draws below stay inside these ranges and needn't reach their ends.
Inputs may be any that keep to these rules, and one draw needn't show every extreme that they name: `part_dest`: among the 32 partial tiles of one device no index of rows is named more than 8 times, and at least one is named exactly 8 times.
All inputs are finite; a program needn't handle non-finite values.
Results may differ from the reference program's by a relative error of at most 0.0022.
Values may be sent and summed in bfloat16 or wider, within the bound.
No kernel may reach another device: no remote copies, remote signals or barrier semaphores. Data moves between devices by JAX's collectives and lax.ppermute only.
A program may use at most 64 MiB of HBM per device.

```python
import math
import jax
import jax.numpy as jnp
import numpy as np
from jax import lax

TILE_SPAN = 64
NIJ = 64
TILES_PER_PART = 4
PAB = 32
OWNR = 16
INTEGRAL_HELD = 128
CD_PAIR_TILES = 32
CAP = 8
PARTIALS_PER_OUT = 8
N_ROWS = 8
N_COLS = 4


def with_ends(drawn, own_key, low, largest):
    longest = drawn.shape.index(max(drawn.shape))
    spots = []
    for shift in (0, 1):
        where = [jax.random.randint(jax.random.fold_in(own_key, axis), (), 0, length) for axis, length in enumerate(drawn.shape)]
        where[longest] = (where[longest] + shift) % drawn.shape[longest]
        spots.append(tuple(where))
    return drawn.at[spots[0]].set(low).at[spots[1]].set(largest)


def block_levels(stream_key, shape, split, least, top_value):
    level = 1.0
    for dim, shards_of in split:
        heights = jax.random.uniform(jax.random.fold_in(jax.random.fold_in(stream_key, 6), dim), (shards_of,), jnp.float32, least / len(split), top_value / len(split))
        level = level * jnp.repeat(jnp.exp(heights), shape[dim] // shards_of).reshape((-1,) + (1,) * (len(shape) - 1 - dim))
    return level


def deal_out(stream_key, own, number, rows, amount, top, reach, skew):
    sequence = jax.random.permutation(stream_key, amount)
    packed, common = load_shares(amount, rows * top, reach, skew, True), load_shares(amount, rows * top, reach, skew, False)
    places = jnp.arange(amount)

    def named(tallies, rotation):
        used = int((tallies > 0).sum())
        fixed = max(1, used // 4)
        passed = fixed + (places - fixed + rotation * (used - fixed)) % max(1, amount - fixed)
        return jnp.zeros((amount,), jnp.int32).at[sequence[jnp.where(places < fixed, places, passed)]].set(jnp.asarray(tallies, jnp.int32))

    tallies = jnp.where(number % 4 == 0, named(packed, number // 4), named(common, number - number // 4 - 1))
    mixed = jax.random.permutation(jax.random.fold_in(own, 3), amount)
    source_of, taker = mixed[0:amount // 2 * 2:2], mixed[1:amount // 2 * 2:2]
    margin = jnp.minimum(tallies[source_of] - 1, reach - tallies[taker]) // 2
    margin = jnp.where((source_of == sequence[0]) | (taker == sequence[0]) | (tallies[taker] == 0), 0, jnp.maximum(margin, 0))
    passed = jax.random.randint(jax.random.fold_in(own, 4), (amount // 2,), 0, 1 << 20) % (margin + 1)
    tallies = tallies.at[source_of].add(-passed).at[taker].add(passed)
    items = jnp.searchsorted(jnp.cumsum(tallies), jnp.arange(rows * top), side="right").astype(jnp.int32)
    grid = items.reshape(top, rows).T
    grid = grid[jax.random.permutation(jax.random.fold_in(own, 1), rows)]
    rotation = jax.random.randint(jax.random.fold_in(own, 2), (rows, 1), 0, top)
    return jnp.take_along_axis(grid, (jnp.arange(top)[None, :] + rotation) % top, axis=1)


def load_shares(amount, total, reach, skew, full):
    portions = [(1 << 20) // math.isqrt(standing ** skew) + 1 for standing in range(1, amount + 1)]
    largest = reach if full else min(reach, max(-(-total // amount), total * portions[0] // sum(portions)))
    least = 1 if total - largest >= amount - 1 else 0
    holding, surplus = [largest] + [least] * (amount - 1), total - largest - least * (amount - 1)
    while surplus > 0:
        candidates = [i for i in range(1, amount) if holding[i] < largest] or [i for i in range(1, amount) if holding[i] < reach]
        mass, budget = sum([portions[i] for i in candidates]), surplus
        for i in candidates:
            more = min(reach - holding[i], max(1, budget * portions[i] // mass), surplus)
            holding[i] = holding[i] + more
            surplus = surplus - more
    return np.array(holding)


def bell_draw(own_key, dims, spread, limit, pieces=(), kind=jnp.bfloat16):
    drawn = spread * jax.random.normal(own_key, dims, jnp.float32)
    if pieces:
        drawn = drawn * block_levels(own_key, dims, pieces, -0.22, 0.18)
    return jnp.clip(drawn, -limit, limit).astype(kind)


def setup_inputs(seed: int = 0) -> dict:
    key_of = jax.random.split(jax.random.key(seed), 7)
    tiles = bell_draw(key_of[0], (N_ROWS * N_COLS * INTEGRAL_HELD, TILE_SPAN * TILE_SPAN), (TILES_PER_PART * TILE_SPAN * PARTIALS_PER_OUT) ** -0.5, 0.125, ((0, 32),))
    integral_cd_tile = with_ends(jax.random.randint(key_of[1], (N_ROWS * N_COLS * INTEGRAL_HELD,), 0, CD_PAIR_TILES), jax.random.fold_in(key_of[1], 1), 0, CD_PAIR_TILES - 1).astype(jnp.int32)
    part_dest_keys = jax.random.split(jax.random.fold_in(key_of[2], 1), (N_ROWS * N_COLS * PAB) // PAB)
    part_dest_turns = jax.random.permutation(jax.random.fold_in(key_of[2], 3), (N_ROWS * N_COLS * PAB) // PAB)
    part_dest = jax.vmap(lambda own, number: deal_out(jax.random.fold_in(key_of[2], 2), own, number, PAB, N_ROWS, 1, CAP, 2))(part_dest_keys, part_dest_turns).reshape((N_ROWS * N_COLS * PAB, 1))
    partial_row_place = with_ends(jax.random.randint(key_of[3], (N_ROWS * N_COLS * PAB,), 0, OWNR), jax.random.fold_in(key_of[3], 1), 0, OWNR - 1).astype(jnp.int32)
    amplitudes = bell_draw(key_of[4], (N_COLS, CD_PAIR_TILES, NIJ * TILE_SPAN), 1.0, 6.0, ((0, 4), (1, 8)))
    residual_in = bell_draw(key_of[5], (N_ROWS, OWNR, NIJ * TILE_SPAN), 1.0, 6.0, ((0, 8), (1, 4)), jnp.float32)
    return dict(tiles=tiles, integral_cd_tile=integral_cd_tile, part_dest=part_dest, partial_row_place=partial_row_place, amplitudes=amplitudes, residual_in=residual_in)


def reference(tiles, integral_cd_tile, part_dest, partial_row_place, amplitudes, residual_in):
    device_count = N_ROWS * N_COLS
    flat_tiles = tiles.reshape(device_count, PAB, TILES_PER_PART, TILE_SPAN, TILE_SPAN)
    flat_cd = integral_cd_tile.reshape(device_count, PAB, TILES_PER_PART)
    target = (part_dest[:, 0] * OWNR + partial_row_place).astype(jnp.int32).reshape(device_count, PAB)

    def advance(summed, position):
        column = position % N_COLS
        panel_rows = lax.dynamic_index_in_dim(amplitudes, column, 0, keepdims=False)
        panel_rows = panel_rows.reshape(CD_PAIR_TILES, NIJ, TILE_SPAN).astype(jnp.float32)
        picked = panel_rows[flat_cd[position]]
        block_list = flat_tiles[position].astype(jnp.float32)
        partial_value = jnp.einsum('ptic,ptac->pia', picked, block_list).reshape(PAB, NIJ * TILE_SPAN)
        rounded = lax.optimization_barrier(partial_value.astype(jnp.bfloat16))
        return summed.at[target[position]].add(rounded.astype(jnp.float32)), None

    start = jnp.zeros((N_ROWS * OWNR, NIJ * TILE_SPAN), jnp.float32)
    summed, _ = lax.scan(advance, start, jnp.arange(device_count, dtype=jnp.int32))
    return residual_in + summed.reshape(N_ROWS, OWNR, NIJ * TILE_SPAN)
```

```python
import functools

import jax
import jax.numpy as jnp
from jax import lax
from jax.experimental import pallas as pl
from jax.experimental.pallas import tpu as pltpu
from jax.sharding import Mesh
from jax.sharding import PartitionSpec as P

SPAN = 64
LANES = 128
PER_PART = 4
OWNR = 16
ROWS_OF_TILE = SPAN * SPAN // LANES
VMEM = pl.BlockSpec(memory_space=pltpu.VMEM)
SMEM = pl.BlockSpec(memory_space=pltpu.SMEM)


def halves_swapped(x):
    return jnp.concatenate([x[:, SPAN:], x[:, :SPAN]], axis=1)


def partial_kernel(cd_ref, amp_ref, tile_ref, out_ref):
    low = lax.broadcasted_iota(jnp.int32, (ROWS_OF_TILE, LANES), 1) < SPAN

    def pair(first, second):
        even = jnp.where(low, first, halves_swapped(second))
        odd = jnp.where(low, halves_swapped(first), second)
        return even, odd

    for q in range(out_ref.shape[0] // ROWS_OF_TILE):
        amps, tiles = [], []
        for t in range(0, PER_PART, 2):
            k = q * PER_PART + t
            amps.append(
                pair(*[
                    amp_ref[
                        pl.ds(pl.multiple_of(cd_ref[k + i] * ROWS_OF_TILE, ROWS_OF_TILE), ROWS_OF_TILE), :
                    ]
                    for i in (0, 1)
                ])
            )
            tiles.append(
                pair(*[tile_ref[pl.ds((k + i) * ROWS_OF_TILE, ROWS_OF_TILE), :] for i in (0, 1)])
            )
        left = jnp.concatenate([jnp.concatenate([a[h] for a in amps], axis=1) for h in (0, 1)], axis=0)
        right = jnp.concatenate([jnp.concatenate([v[h] for v in tiles], axis=1) for h in (0, 1)], axis=0)
        value = lax.dot_general(
            left, right, (((1,), (1,)), ((), ())), preferred_element_type=jnp.float32
        )
        packed = jnp.concatenate([value[:ROWS_OF_TILE], value[ROWS_OF_TILE:]], axis=1)
        out_ref[pl.ds(q * ROWS_OF_TILE, ROWS_OF_TILE), :] = packed.astype(jnp.bfloat16)


def dense_kernel(per_col, pair, own_code_ref, other_code_ref, own_ref, other_ref, out_ref, sum_ref):
    me = lax.axis_index("core")
    groups = OWNR // per_col // pair
    slots = out_ref.shape[0] // ROWS_OF_TILE
    sum_ref[...] = jnp.zeros_like(sum_ref)
    for code_ref, ref in ((own_code_ref, own_ref), (other_code_ref, other_ref)):
        for q in range(ref.shape[0] // ROWS_OF_TILE):
            code = code_ref[q]
            dest, place = code // OWNR, code % OWNR
            col, inner = place // per_col, place % per_col
            slot = (dest * groups + col // pair) * per_col + inner
            slot = jnp.where(col % pair == me, slot, slots)
            at = pl.ds(pl.multiple_of(slot * ROWS_OF_TILE, ROWS_OF_TILE), ROWS_OF_TILE)
            sum_ref[at, :] += ref[pl.ds(q * ROWS_OF_TILE, ROWS_OF_TILE), :].astype(jnp.float32)
    out_ref[...] = sum_ref[pl.ds(0, out_ref.shape[0]), :].astype(jnp.bfloat16)


def final_kernel(in_ref, residual_ref, out_ref, sum_ref):
    total = in_ref[0].astype(jnp.float32)
    for source in range(1, in_ref.shape[0]):
        total += in_ref[source].astype(jnp.float32)
    half = SPAN // 2
    lane = lax.broadcasted_iota(jnp.int32, (LANES, LANES), 0)
    place = lax.broadcasted_iota(jnp.int32, (LANES, LANES), 1)
    target = lane // SPAN * SPAN + lane % half * 2 + lane % SPAN // half
    order = (target == place).astype(jnp.float32)
    sum_ref[...] = jnp.dot(
        total, order, precision=lax.Precision.HIGHEST, preferred_element_type=jnp.float32
    )
    tiles = sum_ref.shape[0] // ROWS_OF_TILE
    for i in range(ROWS_OF_TILE):
        at = pl.ds(i * LANES, LANES)
        out_ref[0, :, at] = residual_ref[0, :, at] + sum_ref[pl.ds(i, tiles, stride=ROWS_OF_TILE), :]


def per_device(rows, groups, pair, tiles, cd_tile, part_dest, place, amplitudes, residual_in):
    held, parts = tiles.shape[0], place.shape[0]
    own_cd = amplitudes.shape[1]
    per_col = residual_in.shape[1]
    bf16, f32 = jnp.bfloat16, jnp.float32
    params = pltpu.CompilerParams(vmem_limit_bytes=48 * 2**20)

    code = part_dest[:, 0] * OWNR + place
    swap = [(i, (i + 1) % pair) for i in range(pair)]
    other_code = lax.ppermute(code, "core", swap)

    shard = amplitudes.reshape(1, own_cd * ROWS_OF_TILE, LANES)
    repeated = jnp.broadcast_to(shard, (rows,) + shard.shape[1:])
    gathered = lax.all_to_all(repeated, "rows", split_axis=0, concat_axis=0, tiled=True)
    gathered = gathered.reshape(rows * own_cd * ROWS_OF_TILE, LANES)

    partial = pl.pallas_call(
        partial_kernel,
        out_shape=jax.ShapeDtypeStruct((parts * ROWS_OF_TILE, LANES), bf16),
        in_specs=[SMEM, VMEM, VMEM],
        out_specs=VMEM,
        compiler_params=params,
    )(cd_tile, gathered, tiles.reshape(held * ROWS_OF_TILE, LANES))

    other = lax.ppermute(partial, "core", swap)
    owners = rows * groups
    dense = pl.pallas_call(
        functools.partial(dense_kernel, per_col, pair),
        out_shape=jax.ShapeDtypeStruct((owners * per_col * ROWS_OF_TILE, LANES), bf16),
        in_specs=[SMEM, SMEM, VMEM, VMEM],
        out_specs=VMEM,
        scratch_shapes=[pltpu.VMEM(((owners * per_col + 1) * ROWS_OF_TILE, LANES), f32)],
        compiler_params=params,
    )(code, other_code, partial, other)

    incoming = lax.all_to_all(
        dense.reshape(owners, per_col * ROWS_OF_TILE, LANES),
        ("rows", "groups"),
        split_axis=0,
        concat_axis=0,
        tiled=True,
    )
    return pl.pallas_call(
        final_kernel,
        out_shape=jax.ShapeDtypeStruct(residual_in.shape, f32),
        in_specs=[VMEM, VMEM],
        out_specs=VMEM,
        scratch_shapes=[pltpu.VMEM((per_col * ROWS_OF_TILE, LANES), f32)],
        compiler_params=params,
    )(incoming, residual_in)


def solution(mesh):
    rows, cols = mesh.shape["rows"], mesh.shape["cols"]
    pair = 2 if cols % 2 == 0 else 1
    split = Mesh(mesh.devices.reshape(rows, cols // pair, pair), ("rows", "groups", "core"))
    every = ("rows", "groups", "core")
    return jax.shard_map(
        functools.partial(per_device, rows, cols // pair, pair),
        mesh=split,
        in_specs=(
            P(every, None),
            P(every),
            P(every, None),
            P(every),
            P(("groups", "core"), "rows", None),
            P("rows", ("groups", "core"), None),
        ),
        out_specs=P("rows", ("groups", "core"), None),
        check_vma=False,
    )
```

```python
import functools

import jax
import jax.numpy as jnp
from jax import lax
from jax.experimental import pallas as pl
from jax.experimental.pallas import tpu as pltpu
from jax.sharding import Mesh
from jax.sharding import PartitionSpec as P

SPAN = 64
LANES = 128
PER_PART = 4
OWNR = 16
ROWS_OF_TILE = SPAN * SPAN // LANES
VMEM = pl.BlockSpec(memory_space=pltpu.VMEM)
SMEM = pl.BlockSpec(memory_space=pltpu.SMEM)


def call(kernel, out_shape, in_specs, *args, scratch=(), aliases=None):
    single = isinstance(out_shape, jax.ShapeDtypeStruct)
    return pl.pallas_call(
        kernel,
        out_shape=out_shape,
        in_specs=in_specs,
        out_specs=VMEM if single else [VMEM] * len(out_shape),
        scratch_shapes=scratch,
        input_output_aliases=aliases or {},
        compiler_params=pltpu.CompilerParams(vmem_limit_bytes=48 * 2**20),
    )(*args)


def tile_rows(first, count=ROWS_OF_TILE):
    return pl.ds(pl.multiple_of(first, ROWS_OF_TILE), count)


def repeat_kernel(in_ref, out_ref, row_ref):
    held = in_ref.shape[1]
    for j in range(ROWS_OF_TILE):
        row_ref[pl.ds(j, held, stride=ROWS_OF_TILE), :] = in_ref[
            0, :, pl.ds(j * LANES, LANES)
        ].astype(jnp.float32)
    rows = row_ref[...].astype(jnp.bfloat16)
    for receiver in range(out_ref.shape[0]):
        out_ref[receiver] = rows


def halves_swapped(x):
    return jnp.concatenate([x[:, SPAN:], x[:, :SPAN]], axis=1)


def pair(low, first, second):
    even = jnp.where(low, first, halves_swapped(second))
    odd = jnp.where(low, halves_swapped(first), second)
    return even, odd


def low_lanes():
    return lax.broadcasted_iota(jnp.int32, (ROWS_OF_TILE, LANES), 1) < SPAN


def pair_kernel(tile_ref, out_ref):
    low = low_lanes()
    for q in range(out_ref.shape[0] // SPAN):
        for t in range(0, PER_PART, 2):
            k = q * PER_PART + t
            halves = pair(
                low, *[tile_ref[pl.ds((k + i) * ROWS_OF_TILE, ROWS_OF_TILE), :] for i in (0, 1)]
            )
            for h in (0, 1):
                at = pl.ds(q * SPAN + h * ROWS_OF_TILE, ROWS_OF_TILE)
                out_ref[at, pl.ds(t * SPAN, LANES)] = halves[h]


def partial_kernel(cd_ref, amp_ref, tile_ref, out_ref):
    low = low_lanes()
    for q in range(out_ref.shape[0] // ROWS_OF_TILE):
        amps = []
        for t in range(0, PER_PART, 2):
            k = q * PER_PART + t
            amps.append(
                pair(low, *[amp_ref[tile_rows(cd_ref[k + i] * ROWS_OF_TILE), :] for i in (0, 1)])
            )
        left = jnp.concatenate([jnp.concatenate([a[h] for a in amps], axis=1) for h in (0, 1)], axis=0)
        value = lax.dot_general(
            left,
            tile_ref[pl.ds(q * SPAN, SPAN), :],
            (((1,), (1,)), ((), ())),
            preferred_element_type=jnp.float32,
        )
        packed = jnp.concatenate([value[:ROWS_OF_TILE], value[ROWS_OF_TILE:]], axis=1)
        out_ref[pl.ds(q * ROWS_OF_TILE, ROWS_OF_TILE), :] = packed.astype(jnp.bfloat16)


def add_tiles(slot_ref, ref, sum_ref):
    for q in range(ref.shape[0] // ROWS_OF_TILE):
        at = tile_rows(slot_ref[q] * ROWS_OF_TILE)
        sum_ref[at, :] += ref[pl.ds(q * ROWS_OF_TILE, ROWS_OF_TILE), :].astype(jnp.float32)


def own_kernel(slot_ref, ref, sum_ref):
    sum_ref[...] = jnp.zeros_like(sum_ref)
    add_tiles(slot_ref, ref, sum_ref)


def other_kernel(slot_ref, ref, in_ref, out_ref, sum_ref):
    add_tiles(slot_ref, ref, sum_ref)
    out_ref[...] = sum_ref[pl.ds(0, out_ref.shape[0]), :].astype(jnp.bfloat16)


def final_kernel(in_ref, residual_ref, out_ref, sum_ref):
    total = in_ref[0].astype(jnp.float32)
    for source in range(1, in_ref.shape[0]):
        total += in_ref[source].astype(jnp.float32)
    half = SPAN // 2
    lane = lax.broadcasted_iota(jnp.int32, (LANES, LANES), 0)
    place = lax.broadcasted_iota(jnp.int32, (LANES, LANES), 1)
    target = lane // SPAN * SPAN + lane % half * 2 + lane % SPAN // half
    order = (target == place).astype(jnp.float32)
    sum_ref[...] = jnp.dot(
        total, order, precision=lax.Precision.HIGHEST, preferred_element_type=jnp.float32
    )
    tiles = sum_ref.shape[0] // ROWS_OF_TILE
    for i in range(ROWS_OF_TILE):
        at = pl.ds(i * LANES, LANES)
        out_ref[0, :, at] = residual_ref[0, :, at] + sum_ref[pl.ds(i, tiles, stride=ROWS_OF_TILE), :]


def per_device(rows, groups, cores, tiles, cd_tile, part_dest, place, amplitudes, residual_in):
    held, parts = tiles.shape[0], place.shape[0]
    own_cd = amplitudes.shape[1]
    per_col = residual_in.shape[1]
    bf16, f32 = jnp.bfloat16, jnp.float32
    shape = jax.ShapeDtypeStruct
    owners = rows * groups
    slots = owners * per_col
    swap = [(i, (i + 1) % cores) for i in range(cores)]

    repeated = call(
        repeat_kernel,
        shape((rows, own_cd * ROWS_OF_TILE, LANES), bf16),
        [VMEM],
        amplitudes,
        scratch=[pltpu.VMEM((own_cd * ROWS_OF_TILE, LANES), f32)],
    )
    gathered = lax.all_to_all(repeated, "rows", split_axis=0, concat_axis=0, tiled=True)

    paired = call(
        pair_kernel,
        shape((parts * SPAN, PER_PART * SPAN), bf16),
        [VMEM],
        tiles.reshape(held * ROWS_OF_TILE, LANES),
    )
    col = place // per_col
    slot = (part_dest[:, 0] * groups + col // cores) * per_col + place % per_col
    stays = col % cores == lax.axis_index("core")
    own_slot = jnp.where(stays, slot, slots)
    if cores > 1:
        other_slot = lax.ppermute(jnp.where(stays, slots, slot), "core", swap)
    else:
        other_slot = jnp.full_like(slot, slots)
    gathered, paired, own_slot, other_slot = lax.optimization_barrier(
        (gathered, paired, own_slot, other_slot)
    )

    partial = call(
        partial_kernel,
        shape((parts * ROWS_OF_TILE, LANES), bf16),
        [SMEM, VMEM, VMEM],
        cd_tile,
        gathered.reshape(rows * own_cd * ROWS_OF_TILE, LANES),
        paired,
    )
    other = lax.ppermute(partial, "core", swap)
    summed = shape(((slots + 1) * ROWS_OF_TILE, LANES), f32)
    own_sum = call(own_kernel, summed, [SMEM, VMEM], own_slot, partial)
    dense, _ = call(
        other_kernel,
        [shape((slots * ROWS_OF_TILE, LANES), bf16), summed],
        [SMEM, VMEM, VMEM],
        other_slot,
        other,
        own_sum,
        aliases={2: 1},
    )
    incoming = lax.all_to_all(
        dense.reshape(owners, per_col * ROWS_OF_TILE, LANES),
        ("rows", "groups"),
        split_axis=0,
        concat_axis=0,
        tiled=True,
    )
    return call(
        final_kernel,
        shape(residual_in.shape, f32),
        [VMEM, VMEM],
        incoming,
        residual_in,
        scratch=[pltpu.VMEM((per_col * ROWS_OF_TILE, LANES), f32)],
    )


def solution(mesh):
    rows, cols = mesh.shape["rows"], mesh.shape["cols"]
    cores = 2 if cols % 2 == 0 else 1
    split = Mesh(mesh.devices.reshape(rows, cols // cores, cores), ("rows", "groups", "core"))
    every = ("rows", "groups", "core")
    return jax.shard_map(
        functools.partial(per_device, rows, cols // cores, cores),
        mesh=split,
        in_specs=(
            P(every, None),
            P(every),
            P(every, None),
            P(every),
            P(("groups", "core"), "rows", None),
            P("rows", ("groups", "core"), None),
        ),
        out_specs=P("rows", ("groups", "core"), None),
        check_vma=False,
    )
```

```python
import functools
import itertools

import jax
import jax.numpy as jnp
from jax import lax
from jax.experimental import pallas as pl
from jax.experimental.pallas import tpu as pltpu
from jax.sharding import Mesh
from jax.sharding import PartitionSpec as P

SPAN = 64
LANES = 128
PER_PART = 4
OWNR = 16
ROWS_OF_TILE = SPAN * SPAN // LANES
MOST_PERMUTED = 4
VMEM = pl.BlockSpec(memory_space=pltpu.VMEM)
SMEM = pl.BlockSpec(memory_space=pltpu.SMEM)


def call(kernel, out_shape, in_specs, *args, scratch=(), aliases=None):
    single = isinstance(out_shape, jax.ShapeDtypeStruct)
    return pl.pallas_call(
        kernel,
        out_shape=out_shape,
        in_specs=in_specs,
        out_specs=VMEM if single else [VMEM] * len(out_shape),
        scratch_shapes=scratch,
        input_output_aliases=aliases or {},
        compiler_params=pltpu.CompilerParams(vmem_limit_bytes=48 * 2**20),
    )(*args)


def tile_rows(first, count=ROWS_OF_TILE):
    return pl.ds(pl.multiple_of(first, ROWS_OF_TILE), count)


def repeat_kernel(in_ref, out_ref, row_ref):
    held = in_ref.shape[1]
    for j in range(ROWS_OF_TILE):
        row_ref[pl.ds(j, held, stride=ROWS_OF_TILE), :] = in_ref[
            0, :, pl.ds(j * LANES, LANES)
        ].astype(jnp.float32)
    rows = row_ref[...].astype(jnp.bfloat16)
    for receiver in range(out_ref.shape[0]):
        out_ref[receiver] = rows


def halves_swapped(x):
    return jnp.concatenate([x[:, SPAN:], x[:, :SPAN]], axis=1)


def pair(low, first, second):
    even = jnp.where(low, first, halves_swapped(second))
    odd = jnp.where(low, halves_swapped(first), second)
    return even, odd


def low_lanes():
    return lax.broadcasted_iota(jnp.int32, (ROWS_OF_TILE, LANES), 1) < SPAN


def pair_kernel(tile_ref, out_ref):
    low = low_lanes()
    for q in range(out_ref.shape[0] // SPAN):
        for t in range(0, PER_PART, 2):
            k = q * PER_PART + t
            halves = pair(
                low, *[tile_ref[pl.ds((k + i) * ROWS_OF_TILE, ROWS_OF_TILE), :] for i in (0, 1)]
            )
            for h in (0, 1):
                at = pl.ds(q * SPAN + h * ROWS_OF_TILE, ROWS_OF_TILE)
                out_ref[at, pl.ds(t * SPAN, LANES)] = halves[h]


def partial_kernel(cd_ref, amp_ref, tile_ref, out_ref):
    low = low_lanes()
    for q in range(out_ref.shape[0] // ROWS_OF_TILE):
        amps = []
        for t in range(0, PER_PART, 2):
            k = q * PER_PART + t
            amps.append(
                pair(low, *[amp_ref[tile_rows(cd_ref[k + i] * ROWS_OF_TILE), :] for i in (0, 1)])
            )
        left = jnp.concatenate([jnp.concatenate([a[h] for a in amps], axis=1) for h in (0, 1)], axis=0)
        value = lax.dot_general(
            left,
            tile_ref[pl.ds(q * SPAN, SPAN), :],
            (((1,), (1,)), ((), ())),
            preferred_element_type=jnp.float32,
        )
        packed = jnp.concatenate([value[:ROWS_OF_TILE], value[ROWS_OF_TILE:]], axis=1)
        out_ref[pl.ds(q * ROWS_OF_TILE, ROWS_OF_TILE), :] = packed.astype(jnp.bfloat16)


def add_tiles(slot_ref, ref, sum_ref):
    for q in range(ref.shape[0] // ROWS_OF_TILE):
        at = tile_rows(slot_ref[q] * ROWS_OF_TILE)
        sum_ref[at, :] += ref[pl.ds(q * ROWS_OF_TILE, ROWS_OF_TILE), :].astype(jnp.float32)


def own_kernel(slot_ref, ref, sum_ref):
    sum_ref[...] = jnp.zeros_like(sum_ref)
    add_tiles(slot_ref, ref, sum_ref)


def other_kernel(slot_ref, ref, in_ref, *refs):
    out_refs, sum_ref = refs[:-1], refs[-1]
    add_tiles(slot_ref, ref, sum_ref)
    for block, out_ref in enumerate(out_refs):
        size = out_ref.shape[0]
        out_ref[...] = sum_ref[pl.ds((block + 1) * size, size), :].astype(jnp.bfloat16)


def plane_kernel(others, own_ref, *refs):
    in_refs, out_refs = refs[:others], refs[others:]
    start = 0
    for out_ref in out_refs:
        at = pl.ds(start, out_ref.shape[0])
        total = own_ref[at, :]
        for ref in in_refs:
            total += ref[at, :].astype(jnp.float32)
        out_ref[...] = total.astype(out_ref.dtype)
        start += out_ref.shape[0]


def final_kernel(*refs):
    in_refs, (residual_ref, out_ref, sum_ref) = refs[:-3], refs[-3:]
    size = sum_ref.shape[0]
    blocks = [
        ref[pl.ds(first, size), :] for ref in in_refs for first in range(0, ref.shape[0], size)
    ]
    total = blocks[0].astype(jnp.float32)
    for block in blocks[1:]:
        total += block.astype(jnp.float32)
    half = SPAN // 2
    lane = lax.broadcasted_iota(jnp.int32, (LANES, LANES), 0)
    place = lax.broadcasted_iota(jnp.int32, (LANES, LANES), 1)
    target = lane // SPAN * SPAN + lane % half * 2 + lane % SPAN // half
    order = (target == place).astype(jnp.float32)
    sum_ref[...] = jnp.dot(
        total, order, precision=lax.Precision.HIGHEST, preferred_element_type=jnp.float32
    )
    tiles = size // ROWS_OF_TILE
    for i in range(ROWS_OF_TILE):
        at = pl.ds(i * LANES, LANES)
        out_ref[0, :, at] = residual_ref[0, :, at] + sum_ref[pl.ds(i, tiles, stride=ROWS_OF_TILE), :]


def shifts(sizes):
    places = list(itertools.product(*map(range, sizes)))
    number = {place: i for i, place in enumerate(places)}
    return [
        [
            (number[p], number[tuple((a + b) % n for a, b, n in zip(p, offset, sizes))])
            for p in places
        ]
        for offset in places[1:]
    ]


def per_device(outer, inner, groups, cores, tiles, cd_tile, part_dest, place, amplitudes, residual_in):
    held, parts = tiles.shape[0], place.shape[0]
    own_cd = amplitudes.shape[1]
    per_col = residual_in.shape[1]
    bf16, f32 = jnp.bfloat16, jnp.float32
    shape = jax.ShapeDtypeStruct
    rows = outer * inner
    plane = inner * groups
    slots = rows * groups * per_col
    by_permutes = outer <= MOST_PERMUTED
    swap = [(i, (i + 1) % cores) for i in range(cores)]

    repeated = call(
        repeat_kernel,
        shape((rows, own_cd * ROWS_OF_TILE, LANES), bf16),
        [VMEM],
        amplitudes,
        scratch=[pltpu.VMEM((own_cd * ROWS_OF_TILE, LANES), f32)],
    )
    gathered = lax.all_to_all(repeated, ("outer", "inner"), split_axis=0, concat_axis=0, tiled=True)

    paired = call(
        pair_kernel,
        shape((parts * SPAN, PER_PART * SPAN), bf16),
        [VMEM],
        tiles.reshape(held * ROWS_OF_TILE, LANES),
    )
    dest, col = part_dest[:, 0], place // per_col
    to_inner = (dest % inner - lax.axis_index("inner")) % inner
    to_group = (col // cores - lax.axis_index("groups")) % groups
    to_outer = dest // inner
    if by_permutes:
        to_outer = (to_outer - lax.axis_index("outer")) % outer
    slot = ((to_inner * groups + to_group) * outer + to_outer) * per_col + place % per_col
    stays = col % cores == lax.axis_index("core")
    own_slot = jnp.where(stays, slot, slots)
    if cores > 1:
        other_slot = lax.ppermute(jnp.where(stays, slots, slot), "core", swap)
    else:
        other_slot = jnp.full_like(slot, slots)
    gathered, paired, own_slot, other_slot = lax.optimization_barrier(
        (gathered, paired, own_slot, other_slot)
    )

    partial = call(
        partial_kernel,
        shape((parts * ROWS_OF_TILE, LANES), bf16),
        [SMEM, VMEM, VMEM],
        cd_tile,
        gathered.reshape(rows * own_cd * ROWS_OF_TILE, LANES),
        paired,
    )
    other = lax.ppermute(partial, "core", swap)
    summed = shape(((slots + 1) * ROWS_OF_TILE, LANES), f32)
    own_sum = call(own_kernel, summed, [SMEM, VMEM], own_slot, partial)
    block = slots // plane * ROWS_OF_TILE
    *leaving, own_sum = call(
        other_kernel,
        [shape((block, LANES), bf16)] * (plane - 1) + [summed],
        [SMEM, VMEM, VMEM],
        other_slot,
        other,
        own_sum,
        aliases={2: plane - 1},
    )
    arrived = [
        lax.ppermute(x, ("inner", "groups"), pairs)
        for x, pairs in zip(leaving, shifts((inner, groups)))
    ]
    mine = per_col * ROWS_OF_TILE
    if by_permutes:
        split = [shape((mine, LANES), f32)] + [shape((mine, LANES), bf16)] * (outer - 1)
    else:
        split = [shape((outer * mine, LANES), bf16)]
    sums = call(
        functools.partial(plane_kernel, len(arrived)),
        split,
        [VMEM] * (1 + len(arrived)),
        own_sum,
        *arrived,
    )
    if by_permutes:
        incoming = [sums[0]] + [
            lax.ppermute(x, "outer", pairs) for x, pairs in zip(sums[1:], shifts((outer,)))
        ]
    else:
        incoming = [
            lax.all_to_all(
                sums[0].reshape(outer, mine, LANES), "outer", split_axis=0, concat_axis=0, tiled=True
            ).reshape(outer * mine, LANES)
        ]
    return call(
        final_kernel,
        shape(residual_in.shape, f32),
        [VMEM] * (len(incoming) + 1),
        *incoming,
        residual_in,
        scratch=[pltpu.VMEM((mine, LANES), f32)],
    )


def solution(mesh):
    rows, cols = mesh.shape["rows"], mesh.shape["cols"]
    inner = 2 if rows % 2 == 0 else 1
    cores = 2 if cols % 2 == 0 else 1
    axes = ("outer", "inner", "groups", "core")
    sizes = (rows // inner, inner, cols // cores, cores)
    split = Mesh(mesh.devices.reshape(sizes), axes)
    return jax.shard_map(
        functools.partial(per_device, *sizes),
        mesh=split,
        in_specs=(
            P(axes, None),
            P(axes),
            P(axes, None),
            P(axes),
            P(axes[2:], axes[:2], None),
            P(axes[:2], axes[2:], None),
        ),
        out_specs=P(axes[:2], axes[2:], None),
        check_vma=False,
    )
```

```python
import functools
import itertools

import jax
import jax.numpy as jnp
from jax import lax
from jax.experimental import pallas as pl
from jax.experimental.pallas import tpu as pltpu
from jax.sharding import Mesh
from jax.sharding import PartitionSpec as P

SPAN = 64
LANES = 128
PER_PART = 4
OWNR = 16
ROWS_OF_TILE = SPAN * SPAN // LANES
MOST_PERMUTED = 4
VMEM = pl.BlockSpec(memory_space=pltpu.VMEM)
SMEM = pl.BlockSpec(memory_space=pltpu.SMEM)


def call(kernel, out_shape, in_specs, *args, scratch=(), aliases=None):
    single = isinstance(out_shape, jax.ShapeDtypeStruct)
    return pl.pallas_call(
        kernel,
        out_shape=out_shape,
        in_specs=in_specs,
        out_specs=VMEM if single else [VMEM] * len(out_shape),
        scratch_shapes=scratch,
        input_output_aliases=aliases or {},
        compiler_params=pltpu.CompilerParams(vmem_limit_bytes=48 * 2**20),
    )(*args)


def tile_rows(first, count=ROWS_OF_TILE):
    return pl.ds(pl.multiple_of(first, ROWS_OF_TILE), count)


def repeat_kernel(in_ref, out_ref, row_ref):
    held = in_ref.shape[1]
    for j in range(ROWS_OF_TILE):
        row_ref[pl.ds(j, held, stride=ROWS_OF_TILE), :] = in_ref[
            0, :, pl.ds(j * LANES, LANES)
        ].astype(jnp.float32)
    rows = row_ref[...].astype(jnp.bfloat16)
    for receiver in range(out_ref.shape[0]):
        out_ref[receiver] = rows


def halves_swapped(x):
    return jnp.concatenate([x[:, SPAN:], x[:, :SPAN]], axis=1)


def pair(low, first, second):
    even = jnp.where(low, first, halves_swapped(second))
    odd = jnp.where(low, halves_swapped(first), second)
    return even, odd


def low_lanes():
    return lax.broadcasted_iota(jnp.int32, (ROWS_OF_TILE, LANES), 1) < SPAN


def pair_kernel(tile_ref, out_ref):
    low = low_lanes()
    for q in range(out_ref.shape[0] // SPAN):
        for t in range(0, PER_PART, 2):
            k = q * PER_PART + t
            halves = pair(
                low, *[tile_ref[pl.ds((k + i) * ROWS_OF_TILE, ROWS_OF_TILE), :] for i in (0, 1)]
            )
            for h in (0, 1):
                at = pl.ds(q * SPAN + h * ROWS_OF_TILE, ROWS_OF_TILE)
                out_ref[at, pl.ds(t * SPAN, LANES)] = halves[h]


def partial_kernel(cd_ref, amp_ref, tile_ref, out_ref):
    low = low_lanes()
    for q in range(out_ref.shape[0] // ROWS_OF_TILE):
        amps = []
        for t in range(0, PER_PART, 2):
            k = q * PER_PART + t
            amps.append(
                pair(low, *[amp_ref[tile_rows(cd_ref[k + i] * ROWS_OF_TILE), :] for i in (0, 1)])
            )
        left = jnp.concatenate([jnp.concatenate([a[h] for a in amps], axis=1) for h in (0, 1)], axis=0)
        value = lax.dot_general(
            left,
            tile_ref[pl.ds(q * SPAN, SPAN), :],
            (((1,), (1,)), ((), ())),
            preferred_element_type=jnp.float32,
        )
        packed = jnp.concatenate([value[:ROWS_OF_TILE], value[ROWS_OF_TILE:]], axis=1)
        out_ref[pl.ds(q * ROWS_OF_TILE, ROWS_OF_TILE), :] = packed.astype(jnp.bfloat16)


def add_tiles(slot_ref, ref, sum_ref):
    for q in range(ref.shape[0] // ROWS_OF_TILE):
        at = tile_rows(slot_ref[q] * ROWS_OF_TILE)
        sum_ref[at, :] += ref[pl.ds(q * ROWS_OF_TILE, ROWS_OF_TILE), :].astype(jnp.float32)


def own_kernel(slot_ref, ref, sum_ref):
    sum_ref[...] = jnp.zeros_like(sum_ref)
    add_tiles(slot_ref, ref, sum_ref)


def other_kernel(slot_ref, ref, in_ref, *refs):
    out_refs, sum_ref = refs[:-1], refs[-1]
    add_tiles(slot_ref, ref, sum_ref)
    for block, out_ref in enumerate(out_refs):
        size = out_ref.shape[0]
        out_ref[...] = sum_ref[pl.ds((block + 1) * size, size), :].astype(jnp.bfloat16)


def plane_kernel(others, own_ref, *refs):
    in_refs, out_refs = refs[:others], refs[others:]
    start = 0
    for out_ref in out_refs:
        at = pl.ds(start, out_ref.shape[0])
        total = own_ref[at, :]
        for ref in in_refs:
            total += ref[at, :].astype(jnp.float32)
        out_ref[...] = total.astype(out_ref.dtype)
        start += out_ref.shape[0]


def final_kernel(*refs):
    in_refs, (residual_ref, out_ref, sum_ref) = refs[:-3], refs[-3:]
    size = sum_ref.shape[0]
    blocks = [
        ref[pl.ds(first, size), :] for ref in in_refs for first in range(0, ref.shape[0], size)
    ]
    total = blocks[0].astype(jnp.float32)
    for block in blocks[1:]:
        total += block.astype(jnp.float32)
    half = SPAN // 2
    lane = lax.broadcasted_iota(jnp.int32, (LANES, LANES), 0)
    place = lax.broadcasted_iota(jnp.int32, (LANES, LANES), 1)
    target = lane // SPAN * SPAN + lane % half * 2 + lane % SPAN // half
    order = (target == place).astype(jnp.float32)
    sum_ref[...] = jnp.dot(
        total, order, precision=lax.Precision.HIGHEST, preferred_element_type=jnp.float32
    )
    tiles = size // ROWS_OF_TILE
    for i in range(ROWS_OF_TILE):
        at = pl.ds(i * LANES, LANES)
        out_ref[0, :, at] = residual_ref[0, :, at] + sum_ref[pl.ds(i, tiles, stride=ROWS_OF_TILE), :]


def offset(to, start, size):
    return to ^ start if size & (size - 1) == 0 else (to - start) % size


def permutes(sizes):
    places = list(itertools.product(*map(range, sizes)))
    number = {place: i for i, place in enumerate(places)}

    def moved(place, by):
        return tuple(
            a ^ b if n & (n - 1) == 0 else (a + b) % n for a, b, n in zip(place, by, sizes)
        )

    return [[(number[p], number[moved(p, by)]) for p in places] for by in places[1:]]


def exchange(blocks, axes, sizes):
    return [lax.ppermute(x, axes, pairs) for x, pairs in zip(blocks, permutes(sizes))][::-1]


def per_device(outer, inner, groups, cores, tiles, cd_tile, part_dest, place, amplitudes, residual_in):
    held, parts = tiles.shape[0], place.shape[0]
    own_cd = amplitudes.shape[1]
    per_col = residual_in.shape[1]
    bf16, f32 = jnp.bfloat16, jnp.float32
    shape = jax.ShapeDtypeStruct
    rows = outer * inner
    plane = inner * groups
    slots = rows * groups * per_col
    by_permutes = outer <= MOST_PERMUTED
    swap = [(i, (i + 1) % cores) for i in range(cores)]

    repeated = call(
        repeat_kernel,
        shape((rows, own_cd * ROWS_OF_TILE, LANES), bf16),
        [VMEM],
        amplitudes,
        scratch=[pltpu.VMEM((own_cd * ROWS_OF_TILE, LANES), f32)],
    )
    gathered = lax.all_to_all(repeated, ("outer", "inner"), split_axis=0, concat_axis=0, tiled=True)

    paired = call(
        pair_kernel,
        shape((parts * SPAN, PER_PART * SPAN), bf16),
        [VMEM],
        tiles.reshape(held * ROWS_OF_TILE, LANES),
    )
    dest, col = part_dest[:, 0], place // per_col
    to_inner = offset(dest % inner, lax.axis_index("inner"), inner)
    to_group = offset(col // cores, lax.axis_index("groups"), groups)
    to_outer = dest // inner
    if by_permutes:
        to_outer = offset(to_outer, lax.axis_index("outer"), outer)
    slot = ((to_inner * groups + to_group) * outer + to_outer) * per_col + place % per_col
    stays = col % cores == lax.axis_index("core")
    own_slot = jnp.where(stays, slot, slots)
    if cores > 1:
        other_slot = lax.ppermute(jnp.where(stays, slots, slot), "core", swap)
    else:
        other_slot = jnp.full_like(slot, slots)
    gathered, paired, own_slot, other_slot = lax.optimization_barrier(
        (gathered, paired, own_slot, other_slot)
    )

    partial = call(
        partial_kernel,
        shape((parts * ROWS_OF_TILE, LANES), bf16),
        [SMEM, VMEM, VMEM],
        cd_tile,
        gathered.reshape(rows * own_cd * ROWS_OF_TILE, LANES),
        paired,
    )
    other = lax.ppermute(partial, "core", swap)
    summed = shape(((slots + 1) * ROWS_OF_TILE, LANES), f32)
    own_sum = call(own_kernel, summed, [SMEM, VMEM], own_slot, partial)
    block = slots // plane * ROWS_OF_TILE
    *leaving, own_sum = call(
        other_kernel,
        [shape((block, LANES), bf16)] * (plane - 1) + [summed],
        [SMEM, VMEM, VMEM],
        other_slot,
        other,
        own_sum,
        aliases={2: plane - 1},
    )
    arrived = exchange(leaving, ("inner", "groups"), (inner, groups))
    mine = per_col * ROWS_OF_TILE
    if by_permutes:
        split = [shape((mine, LANES), f32)] + [shape((mine, LANES), bf16)] * (outer - 1)
    else:
        split = [shape((outer * mine, LANES), bf16)]
    sums = call(
        functools.partial(plane_kernel, len(arrived)),
        split,
        [VMEM] * (1 + len(arrived)),
        own_sum,
        *arrived,
    )
    if by_permutes:
        incoming = exchange(sums[1:], ("outer",), (outer,)) + [sums[0]]
    else:
        incoming = [
            lax.all_to_all(
                sums[0].reshape(outer, mine, LANES), "outer", split_axis=0, concat_axis=0, tiled=True
            ).reshape(outer * mine, LANES)
        ]
    return call(
        final_kernel,
        shape(residual_in.shape, f32),
        [VMEM] * (len(incoming) + 1),
        *incoming,
        residual_in,
        scratch=[pltpu.VMEM((mine, LANES), f32)],
    )


def solution(mesh):
    rows, cols = mesh.shape["rows"], mesh.shape["cols"]
    inner = 2 if rows % 2 == 0 else 1
    cores = 2 if cols % 2 == 0 else 1
    axes = ("outer", "inner", "groups", "core")
    sizes = (rows // inner, inner, cols // cores, cores)
    split = Mesh(mesh.devices.reshape(sizes), axes)
    return jax.shard_map(
        functools.partial(per_device, *sizes),
        mesh=split,
        in_specs=(
            P(axes, None),
            P(axes),
            P(axes, None),
            P(axes),
            P(axes[2:], axes[:2], None),
            P(axes[:2], axes[2:], None),
        ),
        out_specs=P(axes[:2], axes[2:], None),
        check_vma=False,
    )
```

```python
import functools
import itertools

import jax
import jax.numpy as jnp
from jax import lax
from jax.experimental import pallas as pl
from jax.experimental.pallas import tpu as pltpu
from jax.sharding import Mesh
from jax.sharding import PartitionSpec as P

SPAN = 64
LANES = 128
PER_PART = 4
OWNR = 16
ROWS_OF_TILE = SPAN * SPAN // LANES
MOST_PERMUTED = 4
VMEM = pl.BlockSpec(memory_space=pltpu.VMEM)
SMEM = pl.BlockSpec(memory_space=pltpu.SMEM)


def call(kernel, out_shape, in_specs, *args, scratch=(), aliases=None):
    single = isinstance(out_shape, jax.ShapeDtypeStruct)
    return pl.pallas_call(
        kernel,
        out_shape=out_shape,
        in_specs=in_specs,
        out_specs=VMEM if single else [VMEM] * len(out_shape),
        scratch_shapes=scratch,
        input_output_aliases=aliases or {},
        compiler_params=pltpu.CompilerParams(vmem_limit_bytes=48 * 2**20),
    )(*args)


def tile_rows(first, count=ROWS_OF_TILE):
    return pl.ds(pl.multiple_of(first, ROWS_OF_TILE), count)


def offset(to, start, size):
    return to ^ start if size & (size - 1) == 0 else (to - start) % size


def source(by, start, size):
    return start ^ by if size & (size - 1) == 0 else (start - by) % size


def as_rows(in_ref, row_ref):
    held = in_ref.shape[1]
    for j in range(ROWS_OF_TILE):
        row_ref[pl.ds(j, held, stride=ROWS_OF_TILE), :] = in_ref[
            0, :, pl.ds(j * LANES, LANES)
        ].astype(jnp.float32)
    return row_ref[...].astype(jnp.bfloat16)


def layout_kernel(in_ref, out_ref, row_ref):
    out_ref[...] = as_rows(in_ref, row_ref)


def near_kernel(own_ref, *refs):
    in_refs, (out_ref, row_ref) = refs[:-2], refs[-2:]
    size = own_ref.shape[0]
    me = lax.axis_index("inner")
    out_ref[tile_rows(me * size, size), :] = own_ref[...]
    for by, in_ref in enumerate(in_refs):
        at = tile_rows(source(by + 1, me, len(in_refs) + 1) * size, size)
        out_ref[at, :] = as_rows(in_ref, row_ref)


def halves_swapped(x):
    return jnp.concatenate([x[:, SPAN:], x[:, :SPAN]], axis=1)


def pair(low, first, second):
    even = jnp.where(low, first, halves_swapped(second))
    odd = jnp.where(low, halves_swapped(first), second)
    return even, odd


def low_lanes():
    return lax.broadcasted_iota(jnp.int32, (ROWS_OF_TILE, LANES), 1) < SPAN


def pair_kernel(tile_ref, out_ref):
    low = low_lanes()
    for q in range(out_ref.shape[0] // SPAN):
        for t in range(0, PER_PART, 2):
            k = q * PER_PART + t
            halves = pair(
                low, *[tile_ref[pl.ds((k + i) * ROWS_OF_TILE, ROWS_OF_TILE), :] for i in (0, 1)]
            )
            for h in (0, 1):
                at = pl.ds(q * SPAN + h * ROWS_OF_TILE, ROWS_OF_TILE)
                out_ref[at, pl.ds(t * SPAN, LANES)] = halves[h]


def partial_kernel(cd_ref, tile_ref, *refs):
    in_refs, (out_ref, amp_ref) = refs[:-2], refs[-2:]
    low = low_lanes()
    me = lax.axis_index("outer")
    size = in_refs[0].shape[0]
    for by, in_ref in enumerate(reversed(in_refs)):
        amp_ref[tile_rows(source(by, me, len(in_refs)) * size, size), :] = in_ref[...]
    for q in range(out_ref.shape[0] // ROWS_OF_TILE):
        amps = []
        for t in range(0, PER_PART, 2):
            k = q * PER_PART + t
            amps.append(
                pair(low, *[amp_ref[tile_rows(cd_ref[k + i] * ROWS_OF_TILE), :] for i in (0, 1)])
            )
        left = jnp.concatenate([jnp.concatenate([a[h] for a in amps], axis=1) for h in (0, 1)], axis=0)
        value = lax.dot_general(
            left,
            tile_ref[pl.ds(q * SPAN, SPAN), :],
            (((1,), (1,)), ((), ())),
            preferred_element_type=jnp.float32,
        )
        packed = jnp.concatenate([value[:ROWS_OF_TILE], value[ROWS_OF_TILE:]], axis=1)
        out_ref[pl.ds(q * ROWS_OF_TILE, ROWS_OF_TILE), :] = packed.astype(jnp.bfloat16)


def add_tiles(slot_ref, ref, sum_ref):
    for q in range(ref.shape[0] // ROWS_OF_TILE):
        at = tile_rows(slot_ref[q] * ROWS_OF_TILE)
        sum_ref[at, :] += ref[pl.ds(q * ROWS_OF_TILE, ROWS_OF_TILE), :].astype(jnp.float32)


def own_kernel(slot_ref, ref, sum_ref):
    sum_ref[...] = jnp.zeros_like(sum_ref)
    add_tiles(slot_ref, ref, sum_ref)


def other_kernel(slot_ref, ref, in_ref, *refs):
    out_refs, sum_ref = refs[:-1], refs[-1]
    add_tiles(slot_ref, ref, sum_ref)
    for block, out_ref in enumerate(out_refs):
        size = out_ref.shape[0]
        out_ref[...] = sum_ref[pl.ds((block + 1) * size, size), :].astype(jnp.bfloat16)


def plane_kernel(others, own_ref, *refs):
    in_refs, out_refs = refs[:others], refs[others:]
    start = 0
    for out_ref in out_refs:
        at = pl.ds(start, out_ref.shape[0])
        total = own_ref[at, :]
        for ref in in_refs:
            total += ref[at, :].astype(jnp.float32)
        out_ref[...] = total.astype(out_ref.dtype)
        start += out_ref.shape[0]


def final_kernel(*refs):
    in_refs, (residual_ref, out_ref, sum_ref) = refs[:-3], refs[-3:]
    size = sum_ref.shape[0]
    blocks = [
        ref[pl.ds(first, size), :] for ref in in_refs for first in range(0, ref.shape[0], size)
    ]
    total = blocks[0].astype(jnp.float32)
    for block in blocks[1:]:
        total += block.astype(jnp.float32)
    half = SPAN // 2
    lane = lax.broadcasted_iota(jnp.int32, (LANES, LANES), 0)
    place = lax.broadcasted_iota(jnp.int32, (LANES, LANES), 1)
    target = lane // SPAN * SPAN + lane % half * 2 + lane % SPAN // half
    order = (target == place).astype(jnp.float32)
    sum_ref[...] = jnp.dot(
        total, order, precision=lax.Precision.HIGHEST, preferred_element_type=jnp.float32
    )
    tiles = size // ROWS_OF_TILE
    for i in range(ROWS_OF_TILE):
        at = pl.ds(i * LANES, LANES)
        out_ref[0, :, at] = residual_ref[0, :, at] + sum_ref[pl.ds(i, tiles, stride=ROWS_OF_TILE), :]


def permutes(sizes):
    places = list(itertools.product(*map(range, sizes)))
    number = {place: i for i, place in enumerate(places)}

    def moved(place, by):
        return tuple(
            a ^ b if n & (n - 1) == 0 else (a + b) % n for a, b, n in zip(place, by, sizes)
        )

    return [[(number[p], number[moved(p, by)]) for p in places] for by in places[1:]]


def exchange(blocks, axes, sizes):
    return [lax.ppermute(x, axes, pairs) for x, pairs in zip(blocks, permutes(sizes))][::-1]


def per_device(outer, inner, groups, cores, tiles, cd_tile, part_dest, place, amplitudes, residual_in):
    held, parts = tiles.shape[0], place.shape[0]
    own_cd = amplitudes.shape[1]
    per_col = residual_in.shape[1]
    bf16, f32 = jnp.bfloat16, jnp.float32
    shape = jax.ShapeDtypeStruct
    rows = outer * inner
    plane = inner * groups
    slots = rows * groups * per_col
    by_permutes = outer <= MOST_PERMUTED
    swap = [(i, (i + 1) % cores) for i in range(cores)]

    others = exchange([amplitudes] * (inner - 1), ("inner",), (inner,))[::-1]
    shard_rows = own_cd * ROWS_OF_TILE
    row_scratch = [pltpu.VMEM((shard_rows, LANES), f32)]
    own = call(layout_kernel, shape((shard_rows, LANES), bf16), [VMEM], amplitudes, scratch=row_scratch)
    near = call(
        near_kernel,
        shape((inner * shard_rows, LANES), bf16),
        [VMEM] * inner,
        own,
        *others,
        scratch=row_scratch,
    )
    if by_permutes:
        gathered = exchange([near] * (outer - 1), ("outer",), (outer,))[::-1]
    else:
        repeated = jnp.broadcast_to(near, (outer,) + near.shape)
        gathered = lax.all_to_all(repeated, "outer", split_axis=0, concat_axis=0, tiled=True)
        gathered = [gathered.reshape(rows * shard_rows, LANES)]

    paired = call(
        pair_kernel,
        shape((parts * SPAN, PER_PART * SPAN), bf16),
        [VMEM],
        tiles.reshape(held * ROWS_OF_TILE, LANES),
    )
    dest, col = part_dest[:, 0], place // per_col
    to_inner = offset(dest % inner, lax.axis_index("inner"), inner)
    to_group = offset(col // cores, lax.axis_index("groups"), groups)
    to_outer = dest // inner
    if by_permutes:
        to_outer = offset(to_outer, lax.axis_index("outer"), outer)
    slot = ((to_inner * groups + to_group) * outer + to_outer) * per_col + place % per_col
    stays = col % cores == lax.axis_index("core")
    own_slot = jnp.where(stays, slot, slots)
    if cores > 1:
        other_slot = lax.ppermute(jnp.where(stays, slots, slot), "core", swap)
    else:
        other_slot = jnp.full_like(slot, slots)
    gathered, paired, own_slot, other_slot = lax.optimization_barrier(
        (gathered, paired, own_slot, other_slot)
    )

    sources = gathered[::-1] + [near] if by_permutes else gathered
    partial = call(
        partial_kernel,
        shape((parts * ROWS_OF_TILE, LANES), bf16),
        [SMEM] + [VMEM] * (1 + len(sources)),
        cd_tile,
        paired,
        *sources,
        scratch=[pltpu.VMEM((rows * shard_rows, LANES), bf16)],
    )
    other = lax.ppermute(partial, "core", swap)
    summed = shape(((slots + 1) * ROWS_OF_TILE, LANES), f32)
    own_sum = call(own_kernel, summed, [SMEM, VMEM], own_slot, partial)
    block = slots // plane * ROWS_OF_TILE
    *leaving, own_sum = call(
        other_kernel,
        [shape((block, LANES), bf16)] * (plane - 1) + [summed],
        [SMEM, VMEM, VMEM],
        other_slot,
        other,
        own_sum,
        aliases={2: plane - 1},
    )
    arrived = exchange(leaving, ("inner", "groups"), (inner, groups))
    mine = per_col * ROWS_OF_TILE
    if by_permutes:
        split = [shape((mine, LANES), f32)] + [shape((mine, LANES), bf16)] * (outer - 1)
    else:
        split = [shape((outer * mine, LANES), bf16)]
    sums = call(
        functools.partial(plane_kernel, len(arrived)),
        split,
        [VMEM] * (1 + len(arrived)),
        own_sum,
        *arrived,
    )
    if by_permutes:
        incoming = exchange(sums[1:], ("outer",), (outer,)) + [sums[0]]
    else:
        incoming = [
            lax.all_to_all(
                sums[0].reshape(outer, mine, LANES), "outer", split_axis=0, concat_axis=0, tiled=True
            ).reshape(outer * mine, LANES)
        ]
    return call(
        final_kernel,
        shape(residual_in.shape, f32),
        [VMEM] * (len(incoming) + 1),
        *incoming,
        residual_in,
        scratch=[pltpu.VMEM((mine, LANES), f32)],
    )


def solution(mesh):
    rows, cols = mesh.shape["rows"], mesh.shape["cols"]
    inner = 2 if rows % 2 == 0 else 1
    cores = 2 if cols % 2 == 0 else 1
    axes = ("outer", "inner", "groups", "core")
    sizes = (rows // inner, inner, cols // cores, cores)
    split = Mesh(mesh.devices.reshape(sizes), axes)
    return jax.shard_map(
        functools.partial(per_device, *sizes),
        mesh=split,
        in_specs=(
            P(axes, None),
            P(axes),
            P(axes, None),
            P(axes),
            P(axes[2:], axes[:2], None),
            P(axes[:2], axes[2:], None),
        ),
        out_specs=P(axes[:2], axes[2:], None),
        check_vma=False,
    )
```

```python
import functools
import itertools
import math

import jax
import jax.numpy as jnp
from jax import lax
from jax.experimental import pallas as pl
from jax.experimental.pallas import tpu as pltpu
from jax.sharding import Mesh
from jax.sharding import PartitionSpec as P

SPAN = 64
LANES = 128
PER_PART = 4
OWNR = 16
ROWS_OF_TILE = SPAN * SPAN // LANES
MOST_PERMUTED = 4
VMEM = pl.BlockSpec(memory_space=pltpu.VMEM)


def call(kernel, out_shape, in_specs, *args, scratch=(), aliases=None):
    single = isinstance(out_shape, jax.ShapeDtypeStruct)
    return pl.pallas_call(
        kernel,
        out_shape=out_shape,
        in_specs=in_specs,
        out_specs=VMEM if single else [VMEM] * len(out_shape),
        scratch_shapes=scratch,
        input_output_aliases=aliases or {},
        compiler_params=pltpu.CompilerParams(vmem_limit_bytes=48 * 2**20),
    )(*args)


def tile_rows(first, count=ROWS_OF_TILE):
    return pl.ds(pl.multiple_of(first, ROWS_OF_TILE), count)


def offset(to, start, size):
    return to ^ start if size & (size - 1) == 0 else (to - start) % size


def source(by, start, size):
    return start ^ by if size & (size - 1) == 0 else (start - by) % size


def as_rows(in_ref, row_ref):
    held = in_ref.shape[1]
    for j in range(ROWS_OF_TILE):
        row_ref[pl.ds(j, held, stride=ROWS_OF_TILE), :] = in_ref[
            0, :, pl.ds(j * LANES, LANES)
        ].astype(jnp.float32)
    return row_ref[...].astype(jnp.bfloat16)


def down(row):
    size = row.shape[1]
    here = lax.broadcasted_iota(jnp.int32, (size, size), 0) == lax.broadcasted_iota(
        jnp.int32, (size, size), 1
    )
    column = jnp.sum(jnp.where(here, row.astype(jnp.float32), 0.0), axis=1, keepdims=True)
    return jnp.broadcast_to(column.astype(jnp.int32), (size, LANES))


def layout_kernel(sizes, per_col, by_permutes, *refs):
    sources, refs = refs[:4], refs[4:]
    out_ref, first_cd_ref, own_slot_ref, other_slot_ref, row_ref, *local_refs, arrivals = refs
    copies = [
        pltpu.make_async_copy(source_ref, local_ref, arrivals.at[i])
        for i, (source_ref, local_ref) in enumerate(zip(sources, local_refs))
    ]
    for copy in copies:
        copy.start()
    for copy in copies:
        copy.wait()
    in_ref, cd_ref, dest_ref, place_ref = local_refs
    outer, inner, groups, cores = sizes
    out_ref[...] = as_rows(in_ref, row_ref)
    first_cd_ref[...] = down(cd_ref[...] * ROWS_OF_TILE)
    dest, place = dest_ref[...], place_ref[...]
    col = place // per_col
    to_inner = offset(dest % inner, lax.axis_index("inner"), inner)
    to_group = offset(col // cores, lax.axis_index("groups"), groups)
    to_outer = dest // inner
    if by_permutes:
        to_outer = offset(to_outer, lax.axis_index("outer"), outer)
    slot = ((to_inner * groups + to_group) * outer + to_outer) * per_col + place % per_col
    stays = col % cores == lax.axis_index("core")
    unused = math.prod(sizes[:3]) * per_col
    own_slot_ref[...] = down(jnp.where(stays, slot, unused) * ROWS_OF_TILE)
    other_slot_ref[...] = down(jnp.where(stays, unused, slot) * ROWS_OF_TILE)


def near_kernel(own_ref, *refs):
    in_refs, (out_ref, row_ref) = refs[:-2], refs[-2:]
    size = own_ref.shape[0]
    me = lax.axis_index("inner")
    out_ref[tile_rows(me * size, size), :] = own_ref[...]
    for by, in_ref in enumerate(in_refs):
        at = tile_rows(source(by + 1, me, len(in_refs) + 1) * size, size)
        out_ref[at, :] = as_rows(in_ref, row_ref)


def halves_swapped(x):
    return jnp.concatenate([x[:, SPAN:], x[:, :SPAN]], axis=1)


def pair(low, first, second):
    even = jnp.where(low, first, halves_swapped(second))
    odd = jnp.where(low, halves_swapped(first), second)
    return even, odd


def low_lanes():
    return lax.broadcasted_iota(jnp.int32, (ROWS_OF_TILE, LANES), 1) < SPAN


def pair_kernel(tile_ref, out_ref):
    low = low_lanes()
    to = lax.broadcasted_iota(jnp.int32, (SPAN, SPAN), 0)
    row = lax.broadcasted_iota(jnp.int32, (SPAN, SPAN), 1)
    order = (row == to % 2 * ROWS_OF_TILE + to // 2).astype(jnp.bfloat16)
    for q in range(out_ref.shape[0] // SPAN):
        sides = []
        for t in range(0, PER_PART, 2):
            k = q * PER_PART + t
            halves = pair(
                low, *[tile_ref[pl.ds((k + i) * ROWS_OF_TILE, ROWS_OF_TILE), :] for i in (0, 1)]
            )
            sides.append(jnp.concatenate(halves, axis=0))
        both = jnp.concatenate(sides, axis=1)
        ordered = jnp.dot(order, both, preferred_element_type=jnp.float32)
        out_ref[pl.ds(q * SPAN, SPAN), :] = ordered.astype(jnp.bfloat16)


def partial_kernel(cd_ref, tile_ref, *refs):
    in_refs, (out_ref, amp_ref) = refs[:-2], refs[-2:]
    low = low_lanes()
    me = lax.axis_index("outer")
    size = in_refs[0].shape[0]
    for by, in_ref in enumerate(reversed(in_refs)):
        amp_ref[tile_rows(source(by, me, len(in_refs)) * size, size), :] = in_ref[...]
    for q in range(out_ref.shape[0] // ROWS_OF_TILE):
        amps = []
        for t in range(0, PER_PART, 2):
            k = q * PER_PART + t
            amps.append(
                pair(low, *[amp_ref[tile_rows(cd_ref[k + i, 0]), :] for i in (0, 1)])
            )
        left = jnp.concatenate([jnp.concatenate([a[h] for a in amps], axis=1) for h in (0, 1)], axis=0)
        value = lax.dot_general(
            left,
            tile_ref[pl.ds(q * SPAN, SPAN), :],
            (((1,), (1,)), ((), ())),
            preferred_element_type=jnp.float32,
        )
        packed = jnp.concatenate([value[:ROWS_OF_TILE], value[ROWS_OF_TILE:]], axis=1)
        out_ref[pl.ds(q * ROWS_OF_TILE, ROWS_OF_TILE), :] = packed.astype(jnp.bfloat16)


def add_tiles(slot_ref, ref, sum_ref):
    for q in range(ref.shape[0] // ROWS_OF_TILE):
        at = tile_rows(slot_ref[q, 0])
        sum_ref[at, :] += ref[pl.ds(q * ROWS_OF_TILE, ROWS_OF_TILE), :].astype(jnp.float32)


def own_kernel(slot_ref, ref, sum_ref):
    sum_ref[...] = jnp.zeros_like(sum_ref)
    add_tiles(slot_ref, ref, sum_ref)


def other_kernel(slot_ref, ref, in_ref, *refs):
    out_refs, sum_ref = refs[:-1], refs[-1]
    add_tiles(slot_ref, ref, sum_ref)
    for block, out_ref in enumerate(out_refs):
        size = out_ref.shape[0]
        out_ref[...] = sum_ref[pl.ds((block + 1) * size, size), :].astype(jnp.bfloat16)


def plane_kernel(others, own_ref, *refs):
    in_refs, out_refs = refs[:others], refs[others:]
    start = 0
    for out_ref in out_refs:
        at = pl.ds(start, out_ref.shape[0])
        total = own_ref[at, :]
        for ref in in_refs:
            total += ref[at, :].astype(jnp.float32)
        out_ref[...] = total.astype(out_ref.dtype)
        start += out_ref.shape[0]


def final_kernel(*refs):
    in_refs, (residual_ref, out_ref, sum_ref) = refs[:-3], refs[-3:]
    size = sum_ref.shape[0]
    blocks = [
        ref[pl.ds(first, size), :] for ref in in_refs for first in range(0, ref.shape[0], size)
    ]
    total = blocks[0].astype(jnp.float32)
    for block in blocks[1:]:
        total += block.astype(jnp.float32)
    sum_ref[...] = total
    tiles = size // ROWS_OF_TILE
    for i in range(ROWS_OF_TILE):
        at = pl.ds(i * LANES, LANES)
        out_ref[0, :, at] = residual_ref[0, :, at] + sum_ref[pl.ds(i, tiles, stride=ROWS_OF_TILE), :]


def permutes(sizes):
    places = list(itertools.product(*map(range, sizes)))
    number = {place: i for i, place in enumerate(places)}

    def moved(place, by):
        return tuple(
            a ^ b if n & (n - 1) == 0 else (a + b) % n for a, b, n in zip(place, by, sizes)
        )

    return [[(number[p], number[moved(p, by)]) for p in places] for by in places[1:]]


def exchange(blocks, axes, sizes):
    return [lax.ppermute(x, axes, pairs) for x, pairs in zip(blocks, permutes(sizes))][::-1]


def per_device(outer, inner, groups, cores, tiles, cd_tile, part_dest, place, amplitudes, residual_in):
    held, parts = tiles.shape[0], place.shape[0]
    own_cd = amplitudes.shape[1]
    per_col = residual_in.shape[1]
    bf16, f32 = jnp.bfloat16, jnp.float32
    shape = jax.ShapeDtypeStruct
    rows = outer * inner
    plane = inner * groups
    slots = rows * groups * per_col
    by_permutes = outer <= MOST_PERMUTED
    swap = [(i, (i + 1) % cores) for i in range(cores)]

    others = exchange([amplitudes] * (inner - 1), ("inner",), (inner,))[::-1]
    shard_rows = own_cd * ROWS_OF_TILE
    row_scratch = [pltpu.VMEM((shard_rows, LANES), f32)]
    sizes = outer, inner, groups, cores
    rows_of = lambda count: shape((count, LANES), jnp.int32)
    arguments = [
        amplitudes,
        cd_tile.reshape(1, held),
        part_dest.reshape(1, parts),
        place.reshape(1, parts),
    ]
    own, first_cd, own_slot, other_slot = call(
        functools.partial(layout_kernel, sizes, per_col, by_permutes),
        [shape((shard_rows, LANES), bf16), rows_of(held), rows_of(parts), rows_of(parts)],
        [pl.BlockSpec(memory_space=pltpu.HBM)] * len(arguments),
        *[pltpu.with_memory_space_constraint(x, pltpu.HBM) for x in arguments],
        scratch=row_scratch
        + [pltpu.VMEM(x.shape, x.dtype) for x in arguments]
        + [pltpu.SemaphoreType.DMA((len(arguments),))],
    )
    near = call(
        near_kernel,
        shape((inner * shard_rows, LANES), bf16),
        [VMEM] * inner,
        own,
        *others,
        scratch=row_scratch,
    )
    if by_permutes:
        gathered = exchange([near] * (outer - 1), ("outer",), (outer,))[::-1]
    else:
        repeated = jnp.broadcast_to(near, (outer,) + near.shape)
        gathered = lax.all_to_all(repeated, "outer", split_axis=0, concat_axis=0, tiled=True)
        gathered = [gathered.reshape(rows * shard_rows, LANES)]

    paired = call(
        pair_kernel,
        shape((parts * SPAN, PER_PART * SPAN), bf16),
        [VMEM],
        tiles.reshape(held * ROWS_OF_TILE, LANES),
    )
    if cores > 1:
        other_slot = lax.ppermute(other_slot, "core", swap)
    else:
        other_slot = jnp.full_like(other_slot, slots * ROWS_OF_TILE)
    gathered, paired, own_slot, other_slot, first_cd = lax.optimization_barrier(
        (gathered, paired, own_slot, other_slot, first_cd)
    )

    sources = gathered[::-1] + [near] if by_permutes else gathered
    partial = call(
        partial_kernel,
        shape((parts * ROWS_OF_TILE, LANES), bf16),
        [VMEM] * (2 + len(sources)),
        first_cd,
        paired,
        *sources,
        scratch=[pltpu.VMEM((rows * shard_rows, LANES), bf16)],
    )
    other = lax.ppermute(partial, "core", swap)
    summed = shape(((slots + 1) * ROWS_OF_TILE, LANES), f32)
    own_sum = call(own_kernel, summed, [VMEM, VMEM], own_slot, partial)
    block = slots // plane * ROWS_OF_TILE
    *leaving, own_sum = call(
        other_kernel,
        [shape((block, LANES), bf16)] * (plane - 1) + [summed],
        [VMEM, VMEM, VMEM],
        other_slot,
        other,
        own_sum,
        aliases={2: plane - 1},
    )
    arrived = exchange(leaving, ("inner", "groups"), (inner, groups))
    mine = per_col * ROWS_OF_TILE
    if by_permutes:
        split = [shape((mine, LANES), f32)] + [shape((mine, LANES), bf16)] * (outer - 1)
    else:
        split = [shape((outer * mine, LANES), bf16)]
    sums = call(
        functools.partial(plane_kernel, len(arrived)),
        split,
        [VMEM] * (1 + len(arrived)),
        own_sum,
        *arrived,
    )
    if by_permutes:
        incoming = exchange(sums[1:], ("outer",), (outer,)) + [sums[0]]
    else:
        incoming = [
            lax.all_to_all(
                sums[0].reshape(outer, mine, LANES), "outer", split_axis=0, concat_axis=0, tiled=True
            ).reshape(outer * mine, LANES)
        ]
    return call(
        final_kernel,
        shape(residual_in.shape, f32),
        [VMEM] * (len(incoming) + 1),
        *incoming,
        residual_in,
        scratch=[pltpu.VMEM((mine, LANES), f32)],
    )


def solution(mesh):
    rows, cols = mesh.shape["rows"], mesh.shape["cols"]
    inner = 2 if rows % 2 == 0 else 1
    cores = 2 if cols % 2 == 0 else 1
    axes = ("outer", "inner", "groups", "core")
    sizes = (rows // inner, inner, cols // cores, cores)
    split = Mesh(mesh.devices.reshape(sizes), axes)
    return jax.shard_map(
        functools.partial(per_device, *sizes),
        mesh=split,
        in_specs=(
            P(axes, None),
            P(axes),
            P(axes, None),
            P(axes),
            P(axes[2:], axes[:2], None),
            P(axes[:2], axes[2:], None),
        ),
        out_specs=P(axes[:2], axes[2:], None),
        check_vma=False,
    )
```

```python
import functools
import itertools
import math

import jax
import jax.numpy as jnp
from jax import lax
from jax.experimental import pallas as pl
from jax.experimental.pallas import tpu as pltpu
from jax.sharding import Mesh
from jax.sharding import PartitionSpec as P

SPAN = 64
LANES = 128
PER_PART = 4
OWNR = 16
ROWS_OF_TILE = SPAN * SPAN // LANES
MOST_PERMUTED = 4
VMEM = pl.BlockSpec(memory_space=pltpu.VMEM)


def call(kernel, out_shape, in_specs, *args, scratch=(), aliases=None):
    single = isinstance(out_shape, jax.ShapeDtypeStruct)
    return pl.pallas_call(
        kernel,
        out_shape=out_shape,
        in_specs=in_specs,
        out_specs=VMEM if single else [VMEM] * len(out_shape),
        scratch_shapes=scratch,
        input_output_aliases=aliases or {},
        compiler_params=pltpu.CompilerParams(vmem_limit_bytes=48 * 2**20),
    )(*args)


def tile_rows(first, count=ROWS_OF_TILE):
    return pl.ds(pl.multiple_of(first, ROWS_OF_TILE), count)


def offset(to, start, size):
    return to ^ start if size & (size - 1) == 0 else (to - start) % size


def source(by, start, size):
    return start ^ by if size & (size - 1) == 0 else (start - by) % size


def as_rows(in_ref, row_ref):
    held = in_ref.shape[1]
    for j in range(ROWS_OF_TILE):
        row_ref[pl.ds(j, held, stride=ROWS_OF_TILE), :] = in_ref[
            0, :, pl.ds(j * LANES, LANES)
        ].astype(jnp.float32)
    return row_ref[...].astype(jnp.bfloat16)


def down(row):
    size = row.shape[1]
    here = lax.broadcasted_iota(jnp.int32, (size, size), 0) == lax.broadcasted_iota(
        jnp.int32, (size, size), 1
    )
    column = jnp.sum(jnp.where(here, row.astype(jnp.float32), 0.0), axis=1, keepdims=True)
    return jnp.broadcast_to(column.astype(jnp.int32), (size, LANES))


def layout_kernel(sizes, per_col, by_permutes, *refs):
    sources, refs = refs[:4], refs[4:]
    out_ref, first_cd_ref, own_slot_ref, other_slot_ref, row_ref, *local_refs, arrivals = refs
    copies = [
        pltpu.make_async_copy(source_ref, local_ref, arrivals.at[i])
        for i, (source_ref, local_ref) in enumerate(zip(sources, local_refs))
    ]
    for copy in copies:
        copy.start()
    for copy in copies:
        copy.wait()
    in_ref, cd_ref, dest_ref, place_ref = local_refs
    outer, inner, groups, cores = sizes
    out_ref[...] = as_rows(in_ref, row_ref)
    first_cd_ref[...] = down(cd_ref[...] * ROWS_OF_TILE)
    dest, place = dest_ref[...], place_ref[...]
    col = place // per_col
    to_inner = offset(dest % inner, lax.axis_index("inner"), inner)
    to_group = offset(col // cores, lax.axis_index("groups"), groups)
    to_outer = dest // inner
    if by_permutes:
        to_outer = offset(to_outer, lax.axis_index("outer"), outer)
    slot = ((to_inner * groups + to_group) * outer + to_outer) * per_col + place % per_col
    flips = (to_outer != 0).astype(jnp.int32) if by_permutes else 0
    stays = (col + flips) % cores == lax.axis_index("core")
    unused = math.prod(sizes[:3]) * per_col
    own_slot_ref[...] = down(jnp.where(stays, slot, unused) * ROWS_OF_TILE)
    other_slot_ref[...] = down(jnp.where(stays, unused, slot) * ROWS_OF_TILE)


def near_kernel(own_ref, *refs):
    in_refs, (out_ref, row_ref) = refs[:-2], refs[-2:]
    size = own_ref.shape[0]
    me = lax.axis_index("inner")
    out_ref[tile_rows(me * size, size), :] = own_ref[...]
    for by, in_ref in enumerate(in_refs):
        at = tile_rows(source(by + 1, me, len(in_refs) + 1) * size, size)
        out_ref[at, :] = as_rows(in_ref, row_ref)


def halves_swapped(x):
    return jnp.concatenate([x[:, SPAN:], x[:, :SPAN]], axis=1)


def pair(low, first, second):
    even = jnp.where(low, first, halves_swapped(second))
    odd = jnp.where(low, halves_swapped(first), second)
    return even, odd


def low_lanes():
    return lax.broadcasted_iota(jnp.int32, (ROWS_OF_TILE, LANES), 1) < SPAN


def pair_kernel(tile_ref, out_ref):
    low = low_lanes()
    to = lax.broadcasted_iota(jnp.int32, (SPAN, SPAN), 0)
    row = lax.broadcasted_iota(jnp.int32, (SPAN, SPAN), 1)
    order = (row == to % 2 * ROWS_OF_TILE + to // 2).astype(jnp.bfloat16)
    for q in range(out_ref.shape[0] // SPAN):
        sides = []
        for t in range(0, PER_PART, 2):
            k = q * PER_PART + t
            halves = pair(
                low, *[tile_ref[pl.ds((k + i) * ROWS_OF_TILE, ROWS_OF_TILE), :] for i in (0, 1)]
            )
            sides.append(jnp.concatenate(halves, axis=0))
        both = jnp.concatenate(sides, axis=1)
        ordered = jnp.dot(order, both, preferred_element_type=jnp.float32)
        out_ref[pl.ds(q * SPAN, SPAN), :] = ordered.astype(jnp.bfloat16)


def partial_kernel(cd_ref, tile_ref, *refs):
    in_refs, (out_ref, amp_ref) = refs[:-2], refs[-2:]
    low = low_lanes()
    me = lax.axis_index("outer")
    size = in_refs[0].shape[0]
    for by, in_ref in enumerate(reversed(in_refs)):
        amp_ref[tile_rows(source(by, me, len(in_refs)) * size, size), :] = in_ref[...]
    for q in range(out_ref.shape[0] // ROWS_OF_TILE):
        amps = []
        for t in range(0, PER_PART, 2):
            k = q * PER_PART + t
            amps.append(
                pair(low, *[amp_ref[tile_rows(cd_ref[k + i, 0]), :] for i in (0, 1)])
            )
        left = jnp.concatenate([jnp.concatenate([a[h] for a in amps], axis=1) for h in (0, 1)], axis=0)
        value = lax.dot_general(
            left,
            tile_ref[pl.ds(q * SPAN, SPAN), :],
            (((1,), (1,)), ((), ())),
            preferred_element_type=jnp.float32,
        )
        packed = jnp.concatenate([value[:ROWS_OF_TILE], value[ROWS_OF_TILE:]], axis=1)
        out_ref[pl.ds(q * ROWS_OF_TILE, ROWS_OF_TILE), :] = packed.astype(jnp.bfloat16)


def add_tiles(slot_ref, ref, sum_ref):
    for q in range(ref.shape[0] // ROWS_OF_TILE):
        at = tile_rows(slot_ref[q, 0])
        sum_ref[at, :] += ref[pl.ds(q * ROWS_OF_TILE, ROWS_OF_TILE), :].astype(jnp.float32)


def own_kernel(slot_ref, ref, sum_ref):
    sum_ref[...] = jnp.zeros_like(sum_ref)
    add_tiles(slot_ref, ref, sum_ref)


def other_kernel(slot_ref, ref, in_ref, *refs):
    out_refs, sum_ref = refs[:-1], refs[-1]
    add_tiles(slot_ref, ref, sum_ref)
    for block, out_ref in enumerate(out_refs):
        size = out_ref.shape[0]
        out_ref[...] = sum_ref[pl.ds((block + 1) * size, size), :].astype(jnp.bfloat16)


def plane_kernel(others, own_ref, *refs):
    in_refs, out_refs = refs[:others], refs[others:]
    start = 0
    for out_ref in out_refs:
        at = pl.ds(start, out_ref.shape[0])
        total = own_ref[at, :]
        for ref in in_refs:
            total += ref[at, :].astype(jnp.float32)
        out_ref[...] = total.astype(out_ref.dtype)
        start += out_ref.shape[0]


def final_kernel(*refs):
    in_refs, (residual_ref, out_ref, sum_ref) = refs[:-3], refs[-3:]
    size = sum_ref.shape[0]
    blocks = [
        ref[pl.ds(first, size), :] for ref in in_refs for first in range(0, ref.shape[0], size)
    ]
    total = blocks[0].astype(jnp.float32)
    for block in blocks[1:]:
        total += block.astype(jnp.float32)
    sum_ref[...] = total
    tiles = size // ROWS_OF_TILE
    for i in range(ROWS_OF_TILE):
        at = pl.ds(i * LANES, LANES)
        out_ref[0, :, at] = residual_ref[0, :, at] + sum_ref[pl.ds(i, tiles, stride=ROWS_OF_TILE), :]


def permutes(sizes):
    places = list(itertools.product(*map(range, sizes)))
    number = {place: i for i, place in enumerate(places)}

    def moved(place, by):
        return tuple(
            a ^ b if n & (n - 1) == 0 else (a + b) % n for a, b, n in zip(place, by, sizes)
        )

    return {by: [(number[p], number[moved(p, by)]) for p in places] for by in places[1:]}


def exchange(blocks, axes, sizes, flip=0):
    pairs = permutes(sizes)
    offsets = itertools.product(*map(range, sizes[:-1]))
    to = [by + (flip % sizes[-1],) for by in offsets][1:]
    return [lax.ppermute(x, axes, pairs[by]) for x, by in zip(blocks, to)][::-1]


def per_device(outer, inner, groups, cores, tiles, cd_tile, part_dest, place, amplitudes, residual_in):
    held, parts = tiles.shape[0], place.shape[0]
    own_cd = amplitudes.shape[1]
    per_col = residual_in.shape[1]
    bf16, f32 = jnp.bfloat16, jnp.float32
    shape = jax.ShapeDtypeStruct
    rows = outer * inner
    plane = inner * groups
    slots = rows * groups * per_col
    by_permutes = outer <= MOST_PERMUTED
    swap = [(i, (i + 1) % cores) for i in range(cores)]

    others = exchange([amplitudes] * (inner - 1), ("inner", "core"), (inner, cores))[::-1]
    shard_rows = own_cd * ROWS_OF_TILE
    row_scratch = [pltpu.VMEM((shard_rows, LANES), f32)]
    sizes = outer, inner, groups, cores
    rows_of = lambda count: shape((count, LANES), jnp.int32)
    arguments = [
        amplitudes,
        cd_tile.reshape(1, held),
        part_dest.reshape(1, parts),
        place.reshape(1, parts),
    ]
    own, first_cd, own_slot, other_slot = call(
        functools.partial(layout_kernel, sizes, per_col, by_permutes),
        [shape((shard_rows, LANES), bf16), rows_of(held), rows_of(parts), rows_of(parts)],
        [pl.BlockSpec(memory_space=pltpu.HBM)] * len(arguments),
        *[pltpu.with_memory_space_constraint(x, pltpu.HBM) for x in arguments],
        scratch=row_scratch
        + [pltpu.VMEM(x.shape, x.dtype) for x in arguments]
        + [pltpu.SemaphoreType.DMA((len(arguments),))],
    )
    near = call(
        near_kernel,
        shape((inner * shard_rows, LANES), bf16),
        [VMEM] * inner,
        own,
        *others,
        scratch=row_scratch,
    )
    if by_permutes:
        gathered = exchange([near] * (outer - 1), ("outer", "core"), (outer, cores))[::-1]
    else:
        repeated = jnp.broadcast_to(near, (outer,) + near.shape)
        gathered = lax.all_to_all(repeated, "outer", split_axis=0, concat_axis=0, tiled=True)
        gathered = [gathered.reshape(rows * shard_rows, LANES)]

    paired = call(
        pair_kernel,
        shape((parts * SPAN, PER_PART * SPAN), bf16),
        [VMEM],
        tiles.reshape(held * ROWS_OF_TILE, LANES),
    )
    if cores > 1:
        other_slot = lax.ppermute(other_slot, "core", swap)
    else:
        other_slot = jnp.full_like(other_slot, slots * ROWS_OF_TILE)
    gathered, paired, own_slot, other_slot, first_cd = lax.optimization_barrier(
        (gathered, paired, own_slot, other_slot, first_cd)
    )

    sources = gathered[::-1] + [near] if by_permutes else gathered
    partial = call(
        partial_kernel,
        shape((parts * ROWS_OF_TILE, LANES), bf16),
        [VMEM] * (2 + len(sources)),
        first_cd,
        paired,
        *sources,
        scratch=[pltpu.VMEM((rows * shard_rows, LANES), bf16)],
    )
    other = lax.ppermute(partial, "core", swap)
    summed = shape(((slots + 1) * ROWS_OF_TILE, LANES), f32)
    own_sum = call(own_kernel, summed, [VMEM, VMEM], own_slot, partial)
    block = slots // plane * ROWS_OF_TILE
    *leaving, own_sum = call(
        other_kernel,
        [shape((block, LANES), bf16)] * (plane - 1) + [summed],
        [VMEM, VMEM, VMEM],
        other_slot,
        other,
        own_sum,
        aliases={2: plane - 1},
    )
    arrived = exchange(leaving, ("inner", "groups", "core"), (inner, groups, cores))
    mine = per_col * ROWS_OF_TILE
    if by_permutes:
        split = [shape((mine, LANES), f32)] + [shape((mine, LANES), bf16)] * (outer - 1)
    else:
        split = [shape((outer * mine, LANES), bf16)]
    sums = call(
        functools.partial(plane_kernel, len(arrived)),
        split,
        [VMEM] * (1 + len(arrived)),
        own_sum,
        *arrived,
    )
    if by_permutes:
        incoming = exchange(sums[1:], ("outer", "core"), (outer, cores), flip=1) + [sums[0]]
    else:
        incoming = [
            lax.all_to_all(
                sums[0].reshape(outer, mine, LANES), "outer", split_axis=0, concat_axis=0, tiled=True
            ).reshape(outer * mine, LANES)
        ]
    return call(
        final_kernel,
        shape(residual_in.shape, f32),
        [VMEM] * (len(incoming) + 1),
        *incoming,
        residual_in,
        scratch=[pltpu.VMEM((mine, LANES), f32)],
    )


def solution(mesh):
    rows, cols = mesh.shape["rows"], mesh.shape["cols"]
    inner = 2 if rows % 2 == 0 else 1
    cores = 2 if cols % 2 == 0 else 1
    axes = ("outer", "inner", "groups", "core")
    sizes = (rows // inner, inner, cols // cores, cores)
    split = Mesh(mesh.devices.reshape(sizes), axes)
    return jax.shard_map(
        functools.partial(per_device, *sizes),
        mesh=split,
        in_specs=(
            P(axes, None),
            P(axes),
            P(axes, None),
            P(axes),
            P(axes[2:], axes[:2], None),
            P(axes[:2], axes[2:], None),
        ),
        out_specs=P(axes[:2], axes[2:], None),
        check_vma=False,
    )
```

```python
import functools
import itertools
import math

import jax
import jax.numpy as jnp
from jax import lax
from jax.experimental import pallas as pl
from jax.experimental.pallas import tpu as pltpu
from jax.sharding import Mesh
from jax.sharding import PartitionSpec as P

SPAN = 64
LANES = 128
PER_PART = 4
OWNR = 16
ROWS_OF_TILE = SPAN * SPAN // LANES
MOST_PERMUTED = 4
VMEM = pl.BlockSpec(memory_space=pltpu.VMEM)


def call(kernel, out_shape, in_specs, *args, scratch=(), aliases=None):
    single = isinstance(out_shape, jax.ShapeDtypeStruct)
    return pl.pallas_call(
        kernel,
        out_shape=out_shape,
        in_specs=in_specs,
        out_specs=VMEM if single else [VMEM] * len(out_shape),
        scratch_shapes=scratch,
        input_output_aliases=aliases or {},
        compiler_params=pltpu.CompilerParams(vmem_limit_bytes=48 * 2**20),
    )(*args)


def tile_rows(first, count=ROWS_OF_TILE):
    return pl.ds(pl.multiple_of(first, ROWS_OF_TILE), count)


def offset(to, start, size):
    return to ^ start if size & (size - 1) == 0 else (to - start) % size


def source(by, start, size):
    return start ^ by if size & (size - 1) == 0 else (start - by) % size


def as_rows(in_ref, row_ref):
    held = in_ref.shape[1]
    for j in range(ROWS_OF_TILE):
        row_ref[pl.ds(j, held, stride=ROWS_OF_TILE), :] = in_ref[
            0, :, pl.ds(j * LANES, LANES)
        ].astype(jnp.float32)
    return row_ref[...].astype(jnp.bfloat16)


def down(row):
    size = row.shape[1]
    here = lax.broadcasted_iota(jnp.int32, (size, size), 0) == lax.broadcasted_iota(
        jnp.int32, (size, size), 1
    )
    column = jnp.sum(jnp.where(here, row.astype(jnp.float32), 0.0), axis=1, keepdims=True)
    return jnp.broadcast_to(column.astype(jnp.int32), (size, LANES))


def layout_kernel(sizes, per_col, by_permutes, opposite, *refs):
    sources, refs = refs[:4], refs[4:]
    out_ref, first_cd_ref, own_slot_ref, other_slot_ref, row_ref, *local_refs, arrivals = refs
    copies = [
        pltpu.make_async_copy(source_ref, local_ref, arrivals.at[i])
        for i, (source_ref, local_ref) in enumerate(zip(sources, local_refs))
    ]
    for copy in copies:
        copy.start()
    for copy in copies:
        copy.wait()
    in_ref, cd_ref, dest_ref, place_ref = local_refs
    outer, inner, groups, cores = sizes
    out_ref[...] = as_rows(in_ref, row_ref)
    first_cd_ref[...] = down(cd_ref[...] * ROWS_OF_TILE)
    dest, place = dest_ref[...], place_ref[...]
    col = place // per_col
    to_inner = offset(dest % inner, lax.axis_index("inner"), inner)
    to_group = offset(col // cores, lax.axis_index("groups"), groups)
    to_outer = dest // inner
    if by_permutes:
        to_outer = offset(to_outer, lax.axis_index("outer"), outer)
    to_plane = to_inner * groups + to_group

    def slot_on(core):
        plane_first = to_plane * outer + to_outer
        if not opposite:
            return plane_first * per_col + place % per_col
        outer_first = to_outer * (inner * groups) + to_plane
        return jnp.where(core == 0, plane_first, outer_first) * per_col + place % per_col

    me = lax.axis_index("core")
    stays = col % cores == me
    unused = math.prod(sizes[:3]) * per_col
    own_slot_ref[...] = down(jnp.where(stays, slot_on(me), unused) * ROWS_OF_TILE)
    other_slot_ref[...] = down(jnp.where(stays, unused, slot_on(1 - me)) * ROWS_OF_TILE)


def near_kernel(own_ref, *refs):
    in_refs, (out_ref, row_ref) = refs[:-2], refs[-2:]
    size = own_ref.shape[0]
    me = lax.axis_index("inner")
    out_ref[tile_rows(me * size, size), :] = own_ref[...]
    for by, in_ref in enumerate(in_refs):
        at = tile_rows(source(by + 1, me, len(in_refs) + 1) * size, size)
        out_ref[at, :] = as_rows(in_ref, row_ref)


def halves_swapped(x):
    return jnp.concatenate([x[:, SPAN:], x[:, :SPAN]], axis=1)


def pair(low, first, second):
    even = jnp.where(low, first, halves_swapped(second))
    odd = jnp.where(low, halves_swapped(first), second)
    return even, odd


def low_lanes():
    return lax.broadcasted_iota(jnp.int32, (ROWS_OF_TILE, LANES), 1) < SPAN


def pair_kernel(tile_ref, out_ref):
    low = low_lanes()
    to = lax.broadcasted_iota(jnp.int32, (SPAN, SPAN), 0)
    row = lax.broadcasted_iota(jnp.int32, (SPAN, SPAN), 1)
    order = (row == to % 2 * ROWS_OF_TILE + to // 2).astype(jnp.bfloat16)
    for q in range(out_ref.shape[0] // SPAN):
        sides = []
        for t in range(0, PER_PART, 2):
            k = q * PER_PART + t
            halves = pair(
                low, *[tile_ref[pl.ds((k + i) * ROWS_OF_TILE, ROWS_OF_TILE), :] for i in (0, 1)]
            )
            sides.append(jnp.concatenate(halves, axis=0))
        both = jnp.concatenate(sides, axis=1)
        ordered = jnp.dot(order, both, preferred_element_type=jnp.float32)
        out_ref[pl.ds(q * SPAN, SPAN), :] = ordered.astype(jnp.bfloat16)


def partial_kernel(cd_ref, tile_ref, *refs):
    in_refs, (out_ref, amp_ref) = refs[:-2], refs[-2:]
    low = low_lanes()
    me = lax.axis_index("outer")
    size = in_refs[0].shape[0]
    for by, in_ref in enumerate(reversed(in_refs)):
        amp_ref[tile_rows(source(by, me, len(in_refs)) * size, size), :] = in_ref[...]
    for q in range(out_ref.shape[0] // ROWS_OF_TILE):
        amps = []
        for t in range(0, PER_PART, 2):
            k = q * PER_PART + t
            amps.append(
                pair(low, *[amp_ref[tile_rows(cd_ref[k + i, 0]), :] for i in (0, 1)])
            )
        left = jnp.concatenate([jnp.concatenate([a[h] for a in amps], axis=1) for h in (0, 1)], axis=0)
        value = lax.dot_general(
            left,
            tile_ref[pl.ds(q * SPAN, SPAN), :],
            (((1,), (1,)), ((), ())),
            preferred_element_type=jnp.float32,
        )
        packed = jnp.concatenate([value[:ROWS_OF_TILE], value[ROWS_OF_TILE:]], axis=1)
        out_ref[pl.ds(q * ROWS_OF_TILE, ROWS_OF_TILE), :] = packed.astype(jnp.bfloat16)


def add_tiles(slot_ref, ref, sum_ref):
    for q in range(ref.shape[0] // ROWS_OF_TILE):
        at = tile_rows(slot_ref[q, 0])
        sum_ref[at, :] += ref[pl.ds(q * ROWS_OF_TILE, ROWS_OF_TILE), :].astype(jnp.float32)


def own_kernel(slot_ref, ref, sum_ref):
    sum_ref[...] = jnp.zeros_like(sum_ref)
    add_tiles(slot_ref, ref, sum_ref)


def other_kernel(slot_ref, ref, in_ref, *refs):
    out_refs, sum_ref = refs[:-1], refs[-1]
    add_tiles(slot_ref, ref, sum_ref)
    for block, out_ref in enumerate(out_refs):
        size = out_ref.shape[0]
        out_ref[...] = sum_ref[pl.ds((block + 1) * size, size), :].astype(jnp.bfloat16)


def plane_kernel(others, own_ref, *refs):
    in_refs, out_refs = refs[:others], refs[others:]
    start = 0
    for out_ref in out_refs:
        at = pl.ds(start, out_ref.shape[0])
        total = own_ref[at, :]
        for ref in in_refs:
            total += ref[at, :].astype(jnp.float32)
        out_ref[...] = total.astype(out_ref.dtype)
        start += out_ref.shape[0]


def final_kernel(*refs):
    in_refs, (residual_ref, out_ref, sum_ref) = refs[:-3], refs[-3:]
    size = sum_ref.shape[0]
    blocks = [
        ref[pl.ds(first, size), :] for ref in in_refs for first in range(0, ref.shape[0], size)
    ]
    total = blocks[0].astype(jnp.float32)
    for block in blocks[1:]:
        total += block.astype(jnp.float32)
    sum_ref[...] = total
    tiles = size // ROWS_OF_TILE
    for i in range(ROWS_OF_TILE):
        at = pl.ds(i * LANES, LANES)
        out_ref[0, :, at] = residual_ref[0, :, at] + sum_ref[pl.ds(i, tiles, stride=ROWS_OF_TILE), :]


def permutes(sizes):
    places = list(itertools.product(*map(range, sizes)))
    number = {place: i for i, place in enumerate(places)}

    def moved(place, by):
        return tuple(
            a ^ b if n & (n - 1) == 0 else (a + b) % n for a, b, n in zip(place, by, sizes)
        )

    return {by: [(number[p], number[moved(p, by)]) for p in places] for by in places[1:]}


def exchange(blocks, axes, sizes):
    return [lax.ppermute(x, axes, pairs) for x, pairs in zip(blocks, permutes(sizes).values())][::-1]


def exchange_crossed(blocks, sizes, outer_core):
    outer, inner, groups, cores = sizes
    offsets = (
        list(itertools.product(range(outer), [0], [0], [0]))[1:],
        list(itertools.product([0], range(inner), range(groups), [0]))[1:],
    )
    pairs = permutes(sizes)
    arrived = []
    for i, x in enumerate(blocks):
        by_core = [pairs[offsets[core != outer_core][i]] for core in range(cores)]
        both = [by_core[n % cores][n] for n in range(math.prod(sizes))]
        arrived.append(lax.ppermute(x, ("outer", "inner", "groups", "core"), both))
    return arrived[::-1]


def per_device(outer, inner, groups, cores, tiles, cd_tile, part_dest, place, amplitudes, residual_in):
    held, parts = tiles.shape[0], place.shape[0]
    own_cd = amplitudes.shape[1]
    per_col = residual_in.shape[1]
    bf16, f32 = jnp.bfloat16, jnp.float32
    shape = jax.ShapeDtypeStruct
    rows = outer * inner
    plane = inner * groups
    slots = rows * groups * per_col
    by_permutes = outer <= MOST_PERMUTED
    opposite = by_permutes and cores == 2 and outer == plane
    swap = [(i, (i + 1) % cores) for i in range(cores)]

    others = exchange([amplitudes] * (inner - 1), ("inner",), (inner,))[::-1]
    shard_rows = own_cd * ROWS_OF_TILE
    row_scratch = [pltpu.VMEM((shard_rows, LANES), f32)]
    sizes = outer, inner, groups, cores
    rows_of = lambda count: shape((count, LANES), jnp.int32)
    arguments = [
        amplitudes,
        cd_tile.reshape(1, held),
        part_dest.reshape(1, parts),
        place.reshape(1, parts),
    ]
    own, first_cd, own_slot, other_slot = call(
        functools.partial(layout_kernel, sizes, per_col, by_permutes, opposite),
        [shape((shard_rows, LANES), bf16), rows_of(held), rows_of(parts), rows_of(parts)],
        [pl.BlockSpec(memory_space=pltpu.HBM)] * len(arguments),
        *[pltpu.with_memory_space_constraint(x, pltpu.HBM) for x in arguments],
        scratch=row_scratch
        + [pltpu.VMEM(x.shape, x.dtype) for x in arguments]
        + [pltpu.SemaphoreType.DMA((len(arguments),))],
    )
    near = call(
        near_kernel,
        shape((inner * shard_rows, LANES), bf16),
        [VMEM] * inner,
        own,
        *others,
        scratch=row_scratch,
    )
    if by_permutes:
        gathered = exchange([near] * (outer - 1), ("outer",), (outer,))[::-1]
    else:
        repeated = jnp.broadcast_to(near, (outer,) + near.shape)
        gathered = lax.all_to_all(repeated, "outer", split_axis=0, concat_axis=0, tiled=True)
        gathered = [gathered.reshape(rows * shard_rows, LANES)]

    paired = call(
        pair_kernel,
        shape((parts * SPAN, PER_PART * SPAN), bf16),
        [VMEM],
        tiles.reshape(held * ROWS_OF_TILE, LANES),
    )
    if cores > 1:
        other_slot = lax.ppermute(other_slot, "core", swap)
    else:
        other_slot = jnp.full_like(other_slot, slots * ROWS_OF_TILE)
    gathered, paired, own_slot, other_slot, first_cd = lax.optimization_barrier(
        (gathered, paired, own_slot, other_slot, first_cd)
    )

    sources = gathered[::-1] + [near] if by_permutes else gathered
    partial = call(
        partial_kernel,
        shape((parts * ROWS_OF_TILE, LANES), bf16),
        [VMEM] * (2 + len(sources)),
        first_cd,
        paired,
        *sources,
        scratch=[pltpu.VMEM((rows * shard_rows, LANES), bf16)],
    )
    other = lax.ppermute(partial, "core", swap)
    summed = shape(((slots + 1) * ROWS_OF_TILE, LANES), f32)
    own_sum = call(own_kernel, summed, [VMEM, VMEM], own_slot, partial)
    block = slots // plane * ROWS_OF_TILE
    *leaving, own_sum = call(
        other_kernel,
        [shape((block, LANES), bf16)] * (plane - 1) + [summed],
        [VMEM, VMEM, VMEM],
        other_slot,
        other,
        own_sum,
        aliases={2: plane - 1},
    )
    if opposite:
        arrived = exchange_crossed(leaving, sizes, 1)
    else:
        arrived = exchange(leaving, ("inner", "groups"), (inner, groups))
    mine = per_col * ROWS_OF_TILE
    if by_permutes:
        split = [shape((mine, LANES), f32)] + [shape((mine, LANES), bf16)] * (outer - 1)
    else:
        split = [shape((outer * mine, LANES), bf16)]
    sums = call(
        functools.partial(plane_kernel, len(arrived)),
        split,
        [VMEM] * (1 + len(arrived)),
        own_sum,
        *arrived,
    )
    if opposite:
        incoming = exchange_crossed(sums[1:], sizes, 0) + [sums[0]]
    elif by_permutes:
        incoming = exchange(sums[1:], ("outer",), (outer,)) + [sums[0]]
    else:
        incoming = [
            lax.all_to_all(
                sums[0].reshape(outer, mine, LANES), "outer", split_axis=0, concat_axis=0, tiled=True
            ).reshape(outer * mine, LANES)
        ]
    return call(
        final_kernel,
        shape(residual_in.shape, f32),
        [VMEM] * (len(incoming) + 1),
        *incoming,
        residual_in,
        scratch=[pltpu.VMEM((mine, LANES), f32)],
    )


def solution(mesh):
    rows, cols = mesh.shape["rows"], mesh.shape["cols"]
    inner = 2 if rows % 2 == 0 else 1
    cores = 2 if cols % 2 == 0 else 1
    axes = ("outer", "inner", "groups", "core")
    sizes = (rows // inner, inner, cols // cores, cores)
    split = Mesh(mesh.devices.reshape(sizes), axes)
    return jax.shard_map(
        functools.partial(per_device, *sizes),
        mesh=split,
        in_specs=(
            P(axes, None),
            P(axes),
            P(axes, None),
            P(axes),
            P(axes[2:], axes[:2], None),
            P(axes[:2], axes[2:], None),
        ),
        out_specs=P(axes[:2], axes[2:], None),
        check_vma=False,
    )
```

```python
import functools
import itertools
import math

import jax
import jax.numpy as jnp
from jax import lax
from jax.experimental import pallas as pl
from jax.experimental.pallas import tpu as pltpu
from jax.sharding import Mesh
from jax.sharding import PartitionSpec as P

SPAN = 64
LANES = 128
PER_PART = 4
OWNR = 16
ROWS_OF_TILE = SPAN * SPAN // LANES
MOST_PERMUTED = 4
VMEM = pl.BlockSpec(memory_space=pltpu.VMEM)


def call(kernel, out_shape, in_specs, *args, scratch=(), aliases=None):
    single = isinstance(out_shape, jax.ShapeDtypeStruct)
    return pl.pallas_call(
        kernel,
        out_shape=out_shape,
        in_specs=in_specs,
        out_specs=VMEM if single else [VMEM] * len(out_shape),
        scratch_shapes=scratch,
        input_output_aliases=aliases or {},
        compiler_params=pltpu.CompilerParams(vmem_limit_bytes=48 * 2**20),
    )(*args)


def tile_rows(first, count=ROWS_OF_TILE):
    return pl.ds(pl.multiple_of(first, ROWS_OF_TILE), count)


def offset(to, start, size):
    return to ^ start if size & (size - 1) == 0 else (to - start) % size


def source(by, start, size):
    return start ^ by if size & (size - 1) == 0 else (start - by) % size


def as_rows(in_ref, row_ref):
    held = in_ref.shape[1]
    for j in range(ROWS_OF_TILE):
        row_ref[pl.ds(j, held, stride=ROWS_OF_TILE), :] = in_ref[
            0, :, pl.ds(j * LANES, LANES)
        ].astype(jnp.float32)
    return row_ref[...].astype(jnp.bfloat16)


def down(row):
    size = row.shape[1]
    here = lax.broadcasted_iota(jnp.int32, (size, size), 0) == lax.broadcasted_iota(
        jnp.int32, (size, size), 1
    )
    column = jnp.sum(jnp.where(here, row.astype(jnp.float32), 0.0), axis=1, keepdims=True)
    return jnp.broadcast_to(column.astype(jnp.int32), (size, LANES))


def layout_kernel(sizes, per_col, by_permutes, opposite, *refs):
    sources, refs = refs[:4], refs[4:]
    out_ref, first_cd_ref, own_slot_ref, other_slot_ref, row_ref, *local_refs, arrivals = refs
    copies = [
        pltpu.make_async_copy(source_ref, local_ref, arrivals.at[i])
        for i, (source_ref, local_ref) in enumerate(zip(sources, local_refs))
    ]
    for copy in copies:
        copy.start()
    for copy in copies:
        copy.wait()
    in_ref, cd_ref, dest_ref, place_ref = local_refs
    outer, inner, groups, cores = sizes
    out_ref[...] = as_rows(in_ref, row_ref)
    first_cd_ref[...] = down(cd_ref[...] * ROWS_OF_TILE)
    dest, place = dest_ref[...], place_ref[...]
    col = place // per_col
    to_inner = offset(dest % inner, lax.axis_index("inner"), inner)
    to_group = offset(col // cores, lax.axis_index("groups"), groups)
    to_outer = dest // inner
    if by_permutes:
        to_outer = offset(to_outer, lax.axis_index("outer"), outer)
    to_plane = to_inner * groups + to_group

    back = (lax.axis_index("outer") + outer - dest // inner) % outer

    def slot_on(core):
        if not opposite:
            return (to_plane * outer + to_outer) * per_col + place % per_col
        plane_first = to_plane * outer + back
        outer_first = back * (inner * groups) + to_plane
        return jnp.where(core == 0, plane_first, outer_first) * per_col + place % per_col

    me = lax.axis_index("core")
    stays = col % cores == me
    unused = math.prod(sizes[:3]) * per_col
    own_slot_ref[...] = down(jnp.where(stays, slot_on(me), unused) * ROWS_OF_TILE)
    other_slot_ref[...] = down(jnp.where(stays, unused, slot_on(1 - me)) * ROWS_OF_TILE)


def near_kernel(own_ref, *refs):
    in_refs, (out_ref, row_ref) = refs[:-2], refs[-2:]
    size = own_ref.shape[0]
    me = lax.axis_index("inner")
    out_ref[tile_rows(me * size, size), :] = own_ref[...]
    for by, in_ref in enumerate(in_refs):
        at = tile_rows(source(by + 1, me, len(in_refs) + 1) * size, size)
        out_ref[at, :] = as_rows(in_ref, row_ref)


def halves_swapped(x):
    return jnp.concatenate([x[:, SPAN:], x[:, :SPAN]], axis=1)


def pair(low, first, second):
    even = jnp.where(low, first, halves_swapped(second))
    odd = jnp.where(low, halves_swapped(first), second)
    return even, odd


def low_lanes():
    return lax.broadcasted_iota(jnp.int32, (ROWS_OF_TILE, LANES), 1) < SPAN


def pair_kernel(tile_ref, out_ref):
    low = low_lanes()
    to = lax.broadcasted_iota(jnp.int32, (SPAN, SPAN), 0)
    row = lax.broadcasted_iota(jnp.int32, (SPAN, SPAN), 1)
    order = (row == to % 2 * ROWS_OF_TILE + to // 2).astype(jnp.bfloat16)
    for q in range(out_ref.shape[0] // SPAN):
        sides = []
        for t in range(0, PER_PART, 2):
            k = q * PER_PART + t
            halves = pair(
                low, *[tile_ref[pl.ds((k + i) * ROWS_OF_TILE, ROWS_OF_TILE), :] for i in (0, 1)]
            )
            sides.append(jnp.concatenate(halves, axis=0))
        both = jnp.concatenate(sides, axis=1)
        ordered = jnp.dot(order, both, preferred_element_type=jnp.float32)
        out_ref[pl.ds(q * SPAN, SPAN), :] = ordered.astype(jnp.bfloat16)


def partial_kernel(cd_ref, tile_ref, *refs):
    in_refs, (out_ref, amp_ref) = refs[:-2], refs[-2:]
    low = low_lanes()
    me = lax.axis_index("outer")
    size = in_refs[0].shape[0]
    for by, in_ref in enumerate(reversed(in_refs)):
        amp_ref[tile_rows(source(by, me, len(in_refs)) * size, size), :] = in_ref[...]
    for q in range(out_ref.shape[0] // ROWS_OF_TILE):
        amps = []
        for t in range(0, PER_PART, 2):
            k = q * PER_PART + t
            amps.append(
                pair(low, *[amp_ref[tile_rows(cd_ref[k + i, 0]), :] for i in (0, 1)])
            )
        left = jnp.concatenate([jnp.concatenate([a[h] for a in amps], axis=1) for h in (0, 1)], axis=0)
        value = lax.dot_general(
            left,
            tile_ref[pl.ds(q * SPAN, SPAN), :],
            (((1,), (1,)), ((), ())),
            preferred_element_type=jnp.float32,
        )
        packed = jnp.concatenate([value[:ROWS_OF_TILE], value[ROWS_OF_TILE:]], axis=1)
        out_ref[pl.ds(q * ROWS_OF_TILE, ROWS_OF_TILE), :] = packed.astype(jnp.bfloat16)


def add_tiles(slot_ref, ref, sum_ref):
    for q in range(ref.shape[0] // ROWS_OF_TILE):
        at = tile_rows(slot_ref[q, 0])
        sum_ref[at, :] += ref[pl.ds(q * ROWS_OF_TILE, ROWS_OF_TILE), :].astype(jnp.float32)


def own_kernel(slot_ref, ref, sum_ref):
    sum_ref[...] = jnp.zeros_like(sum_ref)
    add_tiles(slot_ref, ref, sum_ref)


def other_kernel(slot_ref, ref, in_ref, *refs):
    out_refs, sum_ref = refs[:-1], refs[-1]
    add_tiles(slot_ref, ref, sum_ref)
    for block, out_ref in enumerate(out_refs):
        size = out_ref.shape[0]
        out_ref[...] = sum_ref[pl.ds((block + 1) * size, size), :].astype(jnp.bfloat16)


def plane_kernel(others, own_ref, *refs):
    in_refs, out_refs = refs[:others], refs[others:]
    start = 0
    for out_ref in out_refs:
        at = pl.ds(start, out_ref.shape[0])
        total = own_ref[at, :]
        for ref in in_refs:
            total += ref[at, :].astype(jnp.float32)
        out_ref[...] = total.astype(out_ref.dtype)
        start += out_ref.shape[0]


def final_kernel(*refs):
    in_refs, (residual_ref, out_ref, sum_ref) = refs[:-3], refs[-3:]
    size = sum_ref.shape[0]
    blocks = [
        ref[pl.ds(first, size), :] for ref in in_refs for first in range(0, ref.shape[0], size)
    ]
    total = blocks[0].astype(jnp.float32)
    for block in blocks[1:]:
        total += block.astype(jnp.float32)
    sum_ref[...] = total
    tiles = size // ROWS_OF_TILE
    for i in range(ROWS_OF_TILE):
        at = pl.ds(i * LANES, LANES)
        out_ref[0, :, at] = residual_ref[0, :, at] + sum_ref[pl.ds(i, tiles, stride=ROWS_OF_TILE), :]


def permutes(sizes):
    places = list(itertools.product(*map(range, sizes)))
    number = {place: i for i, place in enumerate(places)}

    def moved(place, by):
        return tuple(
            a ^ b if n & (n - 1) == 0 else (a + b) % n for a, b, n in zip(place, by, sizes)
        )

    return {by: [(number[p], number[moved(p, by)]) for p in places] for by in places[1:]}


def exchange(blocks, axes, sizes):
    return [lax.ppermute(x, axes, pairs) for x, pairs in zip(blocks, permutes(sizes).values())][::-1]


def exchange_crossed(blocks, sizes, outer_core):
    outer, inner, groups, cores = sizes
    in_plane = [(0, *by, 0) for by in itertools.product(range(inner), range(groups))]
    pairs = permutes(sizes)
    line, total = inner * groups * cores, math.prod(sizes)
    arrived = []
    for i, x in enumerate(blocks, 1):
        across = pairs[in_plane[i]]
        both = [
            (n, (n - i * line) % total) if n % cores == outer_core else across[n] for n in range(total)
        ]
        arrived.append(lax.ppermute(x, ("outer", "inner", "groups", "core"), both))
    return arrived[::-1]


def per_device(outer, inner, groups, cores, tiles, cd_tile, part_dest, place, amplitudes, residual_in):
    held, parts = tiles.shape[0], place.shape[0]
    own_cd = amplitudes.shape[1]
    per_col = residual_in.shape[1]
    bf16, f32 = jnp.bfloat16, jnp.float32
    shape = jax.ShapeDtypeStruct
    rows = outer * inner
    plane = inner * groups
    slots = rows * groups * per_col
    by_permutes = outer <= MOST_PERMUTED
    opposite = by_permutes and cores == 2 and outer == plane
    swap = [(i, (i + 1) % cores) for i in range(cores)]

    others = exchange([amplitudes] * (inner - 1), ("inner",), (inner,))[::-1]
    shard_rows = own_cd * ROWS_OF_TILE
    row_scratch = [pltpu.VMEM((shard_rows, LANES), f32)]
    sizes = outer, inner, groups, cores
    rows_of = lambda count: shape((count, LANES), jnp.int32)
    arguments = [
        amplitudes,
        cd_tile.reshape(1, held),
        part_dest.reshape(1, parts),
        place.reshape(1, parts),
    ]
    own, first_cd, own_slot, other_slot = call(
        functools.partial(layout_kernel, sizes, per_col, by_permutes, opposite),
        [shape((shard_rows, LANES), bf16), rows_of(held), rows_of(parts), rows_of(parts)],
        [pl.BlockSpec(memory_space=pltpu.HBM)] * len(arguments),
        *[pltpu.with_memory_space_constraint(x, pltpu.HBM) for x in arguments],
        scratch=row_scratch
        + [pltpu.VMEM(x.shape, x.dtype) for x in arguments]
        + [pltpu.SemaphoreType.DMA((len(arguments),))],
    )
    near = call(
        near_kernel,
        shape((inner * shard_rows, LANES), bf16),
        [VMEM] * inner,
        own,
        *others,
        scratch=row_scratch,
    )
    if by_permutes:
        gathered = exchange([near] * (outer - 1), ("outer",), (outer,))[::-1]
    else:
        repeated = jnp.broadcast_to(near, (outer,) + near.shape)
        gathered = lax.all_to_all(repeated, "outer", split_axis=0, concat_axis=0, tiled=True)
        gathered = [gathered.reshape(rows * shard_rows, LANES)]

    paired = call(
        pair_kernel,
        shape((parts * SPAN, PER_PART * SPAN), bf16),
        [VMEM],
        tiles.reshape(held * ROWS_OF_TILE, LANES),
    )
    if cores > 1:
        other_slot = lax.ppermute(other_slot, "core", swap)
    else:
        other_slot = jnp.full_like(other_slot, slots * ROWS_OF_TILE)
    gathered, paired, own_slot, other_slot, first_cd = lax.optimization_barrier(
        (gathered, paired, own_slot, other_slot, first_cd)
    )

    sources = gathered[::-1] + [near] if by_permutes else gathered
    partial = call(
        partial_kernel,
        shape((parts * ROWS_OF_TILE, LANES), bf16),
        [VMEM] * (2 + len(sources)),
        first_cd,
        paired,
        *sources,
        scratch=[pltpu.VMEM((rows * shard_rows, LANES), bf16)],
    )
    other = lax.ppermute(partial, "core", swap)
    summed = shape(((slots + 1) * ROWS_OF_TILE, LANES), f32)
    own_sum = call(own_kernel, summed, [VMEM, VMEM], own_slot, partial)
    block = slots // plane * ROWS_OF_TILE
    *leaving, own_sum = call(
        other_kernel,
        [shape((block, LANES), bf16)] * (plane - 1) + [summed],
        [VMEM, VMEM, VMEM],
        other_slot,
        other,
        own_sum,
        aliases={2: plane - 1},
    )
    if opposite:
        arrived = exchange_crossed(leaving, sizes, 1)
    else:
        arrived = exchange(leaving, ("inner", "groups"), (inner, groups))
    mine = per_col * ROWS_OF_TILE
    if by_permutes:
        split = [shape((mine, LANES), f32)] + [shape((mine, LANES), bf16)] * (outer - 1)
    else:
        split = [shape((outer * mine, LANES), bf16)]
    sums = call(
        functools.partial(plane_kernel, len(arrived)),
        split,
        [VMEM] * (1 + len(arrived)),
        own_sum,
        *arrived,
    )
    if opposite:
        incoming = exchange_crossed(sums[1:], sizes, 0) + [sums[0]]
    elif by_permutes:
        incoming = exchange(sums[1:], ("outer",), (outer,)) + [sums[0]]
    else:
        incoming = [
            lax.all_to_all(
                sums[0].reshape(outer, mine, LANES), "outer", split_axis=0, concat_axis=0, tiled=True
            ).reshape(outer * mine, LANES)
        ]
    return call(
        final_kernel,
        shape(residual_in.shape, f32),
        [VMEM] * (len(incoming) + 1),
        *incoming,
        residual_in,
        scratch=[pltpu.VMEM((mine, LANES), f32)],
    )


def solution(mesh):
    rows, cols = mesh.shape["rows"], mesh.shape["cols"]
    inner = 2 if rows % 2 == 0 else 1
    cores = 2 if cols % 2 == 0 else 1
    axes = ("outer", "inner", "groups", "core")
    sizes = (rows // inner, inner, cols // cores, cores)
    split = Mesh(mesh.devices.reshape(sizes), axes)
    return jax.shard_map(
        functools.partial(per_device, *sizes),
        mesh=split,
        in_specs=(
            P(axes, None),
            P(axes),
            P(axes, None),
            P(axes),
            P(axes[2:], axes[:2], None),
            P(axes[:2], axes[2:], None),
        ),
        out_specs=P(axes[:2], axes[2:], None),
        check_vma=False,
    )
```

```python
import functools
import itertools
import math

import jax
import jax.numpy as jnp
from jax import lax
from jax.experimental import pallas as pl
from jax.experimental.pallas import tpu as pltpu
from jax.sharding import Mesh
from jax.sharding import PartitionSpec as P

SPAN = 64
LANES = 128
PER_PART = 4
OWNR = 16
ROWS_OF_TILE = SPAN * SPAN // LANES
MOST_PERMUTED = 4
VMEM = pl.BlockSpec(memory_space=pltpu.VMEM)


def call(kernel, out_shape, in_specs, *args, scratch=(), aliases=None):
    single = isinstance(out_shape, jax.ShapeDtypeStruct)
    return pl.pallas_call(
        kernel,
        out_shape=out_shape,
        in_specs=in_specs,
        out_specs=VMEM if single else [VMEM] * len(out_shape),
        scratch_shapes=scratch,
        input_output_aliases=aliases or {},
        compiler_params=pltpu.CompilerParams(vmem_limit_bytes=48 * 2**20),
    )(*args)


def tile_rows(first, count=ROWS_OF_TILE):
    return pl.ds(pl.multiple_of(first, ROWS_OF_TILE), count)


def offset(to, start, size):
    return to ^ start if size & (size - 1) == 0 else (to - start) % size


def source(by, start, size):
    return start ^ by if size & (size - 1) == 0 else (start - by) % size


def as_rows(in_ref, row_ref):
    held = in_ref.shape[1]
    for j in range(ROWS_OF_TILE):
        row_ref[pl.ds(j, held, stride=ROWS_OF_TILE), :] = in_ref[
            0, :, pl.ds(j * LANES, LANES)
        ].astype(jnp.float32)
    return row_ref[...].astype(jnp.bfloat16)


def down(row):
    size = row.shape[1]
    here = lax.broadcasted_iota(jnp.int32, (size, size), 0) == lax.broadcasted_iota(
        jnp.int32, (size, size), 1
    )
    column = jnp.sum(jnp.where(here, row.astype(jnp.float32), 0.0), axis=1, keepdims=True)
    return jnp.broadcast_to(column.astype(jnp.int32), (size, LANES))


def layout_kernel(sizes, per_col, by_permutes, opposite, *refs):
    sources, refs = refs[:4], refs[4:]
    out_ref, first_cd_ref, own_slot_ref, other_slot_ref, row_ref, *local_refs, arrivals = refs
    copies = [
        pltpu.make_async_copy(source_ref, local_ref, arrivals.at[i])
        for i, (source_ref, local_ref) in enumerate(zip(sources, local_refs))
    ]
    for copy in copies:
        copy.start()
    for copy in copies:
        copy.wait()
    in_ref, cd_ref, dest_ref, place_ref = local_refs
    outer, inner, groups, cores = sizes
    out_ref[...] = as_rows(in_ref, row_ref)
    first_cd_ref[...] = down(cd_ref[...] * ROWS_OF_TILE)
    dest, place = dest_ref[...], place_ref[...]
    col = place // per_col
    to_inner = offset(dest % inner, lax.axis_index("inner"), inner)
    to_group = offset(col // cores, lax.axis_index("groups"), groups)
    to_outer = dest // inner
    if by_permutes:
        to_outer = offset(to_outer, lax.axis_index("outer"), outer)
    to_plane = to_inner * groups + to_group

    back = (lax.axis_index("outer") + outer - dest // inner) % outer

    def slot_on(core):
        if not opposite:
            return (to_plane * outer + to_outer) * per_col + place % per_col
        plane_first = to_plane * outer + back
        outer_first = back * (inner * groups) + to_plane
        return jnp.where(core == 0, plane_first, outer_first) * per_col + place % per_col

    me = lax.axis_index("core")
    stays = col % cores == me
    unused = math.prod(sizes[:3]) * per_col
    own_slot_ref[...] = down(jnp.where(stays, slot_on(me), unused) * ROWS_OF_TILE)
    other_slot_ref[...] = down(jnp.where(stays, unused, slot_on(1 - me)) * ROWS_OF_TILE)


def near_kernel(own_ref, *refs):
    in_refs, (out_ref, row_ref) = refs[:-2], refs[-2:]
    size = own_ref.shape[0]
    me = lax.axis_index("inner")
    out_ref[tile_rows(me * size, size), :] = own_ref[...]
    for by, in_ref in enumerate(in_refs):
        at = tile_rows(source(by + 1, me, len(in_refs) + 1) * size, size)
        out_ref[at, :] = as_rows(in_ref, row_ref)


def halves_swapped(x):
    return jnp.concatenate([x[:, SPAN:], x[:, :SPAN]], axis=1)


def pair(low, first, second):
    even = jnp.where(low, first, halves_swapped(second))
    odd = jnp.where(low, halves_swapped(first), second)
    return even, odd


def low_lanes():
    return lax.broadcasted_iota(jnp.int32, (ROWS_OF_TILE, LANES), 1) < SPAN


def pair_kernel(tile_ref, out_ref):
    low = low_lanes()
    to = lax.broadcasted_iota(jnp.int32, (SPAN, SPAN), 0)
    row = lax.broadcasted_iota(jnp.int32, (SPAN, SPAN), 1)
    order = (row == to % 2 * ROWS_OF_TILE + to // 2).astype(jnp.bfloat16)
    for q in range(out_ref.shape[0] // SPAN):
        sides = []
        for t in range(0, PER_PART, 2):
            k = q * PER_PART + t
            halves = pair(
                low, *[tile_ref[pl.ds((k + i) * ROWS_OF_TILE, ROWS_OF_TILE), :] for i in (0, 1)]
            )
            sides.append(jnp.concatenate(halves, axis=0))
        both = jnp.concatenate(sides, axis=1)
        ordered = jnp.dot(order, both, preferred_element_type=jnp.float32)
        out_ref[pl.ds(q * SPAN, SPAN), :] = ordered.astype(jnp.bfloat16)


def partial_kernel(cd_ref, tile_ref, *refs):
    in_refs, (first_ref, second_ref, amp_ref) = refs[:-3], refs[-3:]
    low = low_lanes()
    me = lax.axis_index("outer")
    size = in_refs[0].shape[0]
    for by, in_ref in enumerate(reversed(in_refs)):
        amp_ref[tile_rows(source(by, me, len(in_refs)) * size, size), :] = in_ref[...]
    half = first_ref.shape[0] // ROWS_OF_TILE
    for q in range(2 * half):
        amps = []
        for t in range(0, PER_PART, 2):
            k = q * PER_PART + t
            amps.append(
                pair(low, *[amp_ref[tile_rows(cd_ref[k + i, 0]), :] for i in (0, 1)])
            )
        left = jnp.concatenate([jnp.concatenate([a[h] for a in amps], axis=1) for h in (0, 1)], axis=0)
        value = lax.dot_general(
            left,
            tile_ref[pl.ds(q * SPAN, SPAN), :],
            (((1,), (1,)), ((), ())),
            preferred_element_type=jnp.float32,
        )
        packed = jnp.concatenate([value[:ROWS_OF_TILE], value[ROWS_OF_TILE:]], axis=1)
        out_ref = first_ref if q < half else second_ref
        out_ref[pl.ds(q % half * ROWS_OF_TILE, ROWS_OF_TILE), :] = packed.astype(jnp.bfloat16)


def add_tiles(slot_ref, ref, sum_ref, start=0):
    for q in range(ref.shape[0] // ROWS_OF_TILE):
        at = tile_rows(slot_ref[start + q, 0])
        sum_ref[at, :] += ref[pl.ds(q * ROWS_OF_TILE, ROWS_OF_TILE), :].astype(jnp.float32)


def own_kernel(slot_ref, first_ref, second_ref, sum_ref):
    sum_ref[...] = jnp.zeros_like(sum_ref)
    add_tiles(slot_ref, first_ref, sum_ref)
    add_tiles(slot_ref, second_ref, sum_ref, first_ref.shape[0] // ROWS_OF_TILE)


def half_kernel(slot_ref, ref, in_ref, sum_ref):
    add_tiles(slot_ref, ref, sum_ref)


def other_kernel(slot_ref, ref, in_ref, *refs):
    out_refs, sum_ref = refs[:-1], refs[-1]
    add_tiles(slot_ref, ref, sum_ref, ref.shape[0] // ROWS_OF_TILE)
    for block, out_ref in enumerate(out_refs):
        size = out_ref.shape[0]
        out_ref[...] = sum_ref[pl.ds((block + 1) * size, size), :].astype(jnp.bfloat16)


def plane_kernel(others, own_ref, *refs):
    in_refs, out_refs = refs[:others], refs[others:]
    start = 0
    for out_ref in out_refs:
        at = pl.ds(start, out_ref.shape[0])
        total = own_ref[at, :]
        for ref in in_refs:
            total += ref[at, :].astype(jnp.float32)
        out_ref[...] = total.astype(out_ref.dtype)
        start += out_ref.shape[0]


def final_kernel(*refs):
    in_refs, (residual_ref, out_ref, sum_ref) = refs[:-3], refs[-3:]
    size = sum_ref.shape[0]
    blocks = [
        ref[pl.ds(first, size), :] for ref in in_refs for first in range(0, ref.shape[0], size)
    ]
    total = blocks[0].astype(jnp.float32)
    for block in blocks[1:]:
        total += block.astype(jnp.float32)
    sum_ref[...] = total
    tiles = size // ROWS_OF_TILE
    for i in range(ROWS_OF_TILE):
        at = pl.ds(i * LANES, LANES)
        out_ref[0, :, at] = residual_ref[0, :, at] + sum_ref[pl.ds(i, tiles, stride=ROWS_OF_TILE), :]


def permutes(sizes):
    places = list(itertools.product(*map(range, sizes)))
    number = {place: i for i, place in enumerate(places)}

    def moved(place, by):
        return tuple(
            a ^ b if n & (n - 1) == 0 else (a + b) % n for a, b, n in zip(place, by, sizes)
        )

    return {by: [(number[p], number[moved(p, by)]) for p in places] for by in places[1:]}


def exchange(blocks, axes, sizes):
    return [lax.ppermute(x, axes, pairs) for x, pairs in zip(blocks, permutes(sizes).values())][::-1]


def exchange_crossed(blocks, sizes, outer_core):
    outer, inner, groups, cores = sizes
    in_plane = [(0, *by, 0) for by in itertools.product(range(inner), range(groups))]
    pairs = permutes(sizes)
    line, total = inner * groups * cores, math.prod(sizes)
    arrived = []
    for i, x in enumerate(blocks, 1):
        across = pairs[in_plane[i]]
        both = [
            (n, (n - i * line) % total) if n % cores == outer_core else across[n] for n in range(total)
        ]
        arrived.append(lax.ppermute(x, ("outer", "inner", "groups", "core"), both))
    return arrived[::-1]


def per_device(outer, inner, groups, cores, tiles, cd_tile, part_dest, place, amplitudes, residual_in):
    held, parts = tiles.shape[0], place.shape[0]
    own_cd = amplitudes.shape[1]
    per_col = residual_in.shape[1]
    bf16, f32 = jnp.bfloat16, jnp.float32
    shape = jax.ShapeDtypeStruct
    rows = outer * inner
    plane = inner * groups
    slots = rows * groups * per_col
    by_permutes = outer <= MOST_PERMUTED
    opposite = by_permutes and cores == 2 and outer == plane
    swap = [(i, (i + 1) % cores) for i in range(cores)]

    others = exchange([amplitudes] * (inner - 1), ("inner",), (inner,))[::-1]
    shard_rows = own_cd * ROWS_OF_TILE
    row_scratch = [pltpu.VMEM((shard_rows, LANES), f32)]
    sizes = outer, inner, groups, cores
    rows_of = lambda count: shape((count, LANES), jnp.int32)
    arguments = [
        amplitudes,
        cd_tile.reshape(1, held),
        part_dest.reshape(1, parts),
        place.reshape(1, parts),
    ]
    own, first_cd, own_slot, other_slot = call(
        functools.partial(layout_kernel, sizes, per_col, by_permutes, opposite),
        [shape((shard_rows, LANES), bf16), rows_of(held), rows_of(parts), rows_of(parts)],
        [pl.BlockSpec(memory_space=pltpu.HBM)] * len(arguments),
        *[pltpu.with_memory_space_constraint(x, pltpu.HBM) for x in arguments],
        scratch=row_scratch
        + [pltpu.VMEM(x.shape, x.dtype) for x in arguments]
        + [pltpu.SemaphoreType.DMA((len(arguments),))],
    )
    near = call(
        near_kernel,
        shape((inner * shard_rows, LANES), bf16),
        [VMEM] * inner,
        own,
        *others,
        scratch=row_scratch,
    )
    if by_permutes:
        gathered = exchange([near] * (outer - 1), ("outer",), (outer,))[::-1]
    else:
        repeated = jnp.broadcast_to(near, (outer,) + near.shape)
        gathered = lax.all_to_all(repeated, "outer", split_axis=0, concat_axis=0, tiled=True)
        gathered = [gathered.reshape(rows * shard_rows, LANES)]

    paired = call(
        pair_kernel,
        shape((parts * SPAN, PER_PART * SPAN), bf16),
        [VMEM],
        tiles.reshape(held * ROWS_OF_TILE, LANES),
    )
    if cores > 1:
        other_slot = lax.ppermute(other_slot, "core", swap)
    else:
        other_slot = jnp.full_like(other_slot, slots * ROWS_OF_TILE)
    gathered, paired, own_slot, other_slot, first_cd = lax.optimization_barrier(
        (gathered, paired, own_slot, other_slot, first_cd)
    )

    sources = gathered[::-1] + [near] if by_permutes else gathered
    partial = call(
        partial_kernel,
        [shape((parts // 2 * ROWS_OF_TILE, LANES), bf16)] * 2,
        [VMEM] * (2 + len(sources)),
        first_cd,
        paired,
        *sources,
        scratch=[pltpu.VMEM((rows * shard_rows, LANES), bf16)],
    )
    other = [lax.ppermute(x, "core", swap) for x in partial]
    summed = shape(((slots + 1) * ROWS_OF_TILE, LANES), f32)
    own_sum = call(own_kernel, summed, [VMEM] * 3, own_slot, *partial)
    own_sum = call(half_kernel, summed, [VMEM] * 3, other_slot, other[0], own_sum, aliases={2: 0})
    block = slots // plane * ROWS_OF_TILE
    *leaving, own_sum = call(
        other_kernel,
        [shape((block, LANES), bf16)] * (plane - 1) + [summed],
        [VMEM, VMEM, VMEM],
        other_slot,
        other[1],
        own_sum,
        aliases={2: plane - 1},
    )
    if opposite:
        arrived = exchange_crossed(leaving, sizes, 1)
    else:
        arrived = exchange(leaving, ("inner", "groups"), (inner, groups))
    mine = per_col * ROWS_OF_TILE
    if by_permutes:
        split = [shape((mine, LANES), f32)] + [shape((mine, LANES), bf16)] * (outer - 1)
    else:
        split = [shape((outer * mine, LANES), bf16)]
    sums = call(
        functools.partial(plane_kernel, len(arrived)),
        split,
        [VMEM] * (1 + len(arrived)),
        own_sum,
        *arrived,
    )
    if opposite:
        incoming = exchange_crossed(sums[1:], sizes, 0) + [sums[0]]
    elif by_permutes:
        incoming = exchange(sums[1:], ("outer",), (outer,)) + [sums[0]]
    else:
        incoming = [
            lax.all_to_all(
                sums[0].reshape(outer, mine, LANES), "outer", split_axis=0, concat_axis=0, tiled=True
            ).reshape(outer * mine, LANES)
        ]
    return call(
        final_kernel,
        shape(residual_in.shape, f32),
        [VMEM] * (len(incoming) + 1),
        *incoming,
        residual_in,
        scratch=[pltpu.VMEM((mine, LANES), f32)],
    )


def solution(mesh):
    rows, cols = mesh.shape["rows"], mesh.shape["cols"]
    inner = 2 if rows % 2 == 0 else 1
    cores = 2 if cols % 2 == 0 else 1
    axes = ("outer", "inner", "groups", "core")
    sizes = (rows // inner, inner, cols // cores, cores)
    split = Mesh(mesh.devices.reshape(sizes), axes)
    return jax.shard_map(
        functools.partial(per_device, *sizes),
        mesh=split,
        in_specs=(
            P(axes, None),
            P(axes),
            P(axes, None),
            P(axes),
            P(axes[2:], axes[:2], None),
            P(axes[:2], axes[2:], None),
        ),
        out_specs=P(axes[:2], axes[2:], None),
        check_vma=False,
    )
```

```python
import functools
import itertools
import math

import jax
import jax.numpy as jnp
from jax import lax
from jax.experimental import pallas as pl
from jax.experimental.pallas import tpu as pltpu
from jax.sharding import Mesh
from jax.sharding import PartitionSpec as P

SPAN = 64
LANES = 128
PER_PART = 4
OWNR = 16
ROWS_OF_TILE = SPAN * SPAN // LANES
MOST_PERMUTED = 4
VMEM = pl.BlockSpec(memory_space=pltpu.VMEM)


def call(kernel, out_shape, in_specs, *args, scratch=(), aliases=None):
    single = isinstance(out_shape, jax.ShapeDtypeStruct)
    return pl.pallas_call(
        kernel,
        out_shape=out_shape,
        in_specs=in_specs,
        out_specs=VMEM if single else [VMEM] * len(out_shape),
        scratch_shapes=scratch,
        input_output_aliases=aliases or {},
        compiler_params=pltpu.CompilerParams(vmem_limit_bytes=48 * 2**20),
    )(*args)


def tile_rows(first, count=ROWS_OF_TILE):
    return pl.ds(pl.multiple_of(first, ROWS_OF_TILE), count)


def offset(to, start, size):
    return to ^ start if size & (size - 1) == 0 else (to - start) % size


def source(by, start, size):
    return start ^ by if size & (size - 1) == 0 else (start - by) % size


def as_rows(in_ref, row_ref):
    held = in_ref.shape[1]
    for j in range(ROWS_OF_TILE):
        row_ref[pl.ds(j, held, stride=ROWS_OF_TILE), :] = in_ref[
            0, :, pl.ds(j * LANES, LANES)
        ].astype(jnp.float32)
    return row_ref[...].astype(jnp.bfloat16)


def down(row):
    size = row.shape[1]
    here = lax.broadcasted_iota(jnp.int32, (size, size), 0) == lax.broadcasted_iota(
        jnp.int32, (size, size), 1
    )
    column = jnp.sum(jnp.where(here, row.astype(jnp.float32), 0.0), axis=1, keepdims=True)
    return jnp.broadcast_to(column.astype(jnp.int32), (size, LANES))


def layout_kernel(sizes, per_col, by_permutes, opposite, *refs):
    sources, refs = refs[:4], refs[4:]
    out_ref, first_cd_ref, own_slot_ref, other_slot_ref, row_ref, *local_refs, arrivals = refs
    copies = [
        pltpu.make_async_copy(source_ref, local_ref, arrivals.at[i])
        for i, (source_ref, local_ref) in enumerate(zip(sources, local_refs))
    ]
    for copy in copies:
        copy.start()
    for copy in copies:
        copy.wait()
    in_ref, cd_ref, dest_ref, place_ref = local_refs
    outer, inner, groups, cores = sizes
    out_ref[...] = as_rows(in_ref, row_ref)
    first_cd_ref[...] = down(cd_ref[...] * ROWS_OF_TILE)
    dest, place = dest_ref[...], place_ref[...]
    col = place // per_col
    to_inner = offset(dest % inner, lax.axis_index("inner"), inner)
    to_group = offset(col // cores, lax.axis_index("groups"), groups)
    to_outer = dest // inner
    if by_permutes:
        to_outer = offset(to_outer, lax.axis_index("outer"), outer)
    to_plane = to_inner * groups + to_group

    back = (lax.axis_index("outer") + outer - dest // inner) % outer

    def slot_on(core):
        if not opposite:
            return (to_plane * outer + to_outer) * per_col + place % per_col
        swapped = to_inner + groups * to_group
        plane_first = swapped * outer + back
        outer_first = back * (inner * groups) + to_plane
        return jnp.where(core == 0, plane_first, outer_first) * per_col + place % per_col

    me = lax.axis_index("core")
    stays = col % cores == me
    unused = math.prod(sizes[:3]) * per_col
    own_slot_ref[...] = down(jnp.where(stays, slot_on(me), unused) * ROWS_OF_TILE)
    other_slot_ref[...] = down(jnp.where(stays, unused, slot_on(1 - me)) * ROWS_OF_TILE)


def near_kernel(own_ref, *refs):
    in_refs, (out_ref, row_ref) = refs[:-2], refs[-2:]
    size = own_ref.shape[0]
    me = lax.axis_index("inner")
    out_ref[tile_rows(me * size, size), :] = own_ref[...]
    for by, in_ref in enumerate(in_refs):
        at = tile_rows(source(by + 1, me, len(in_refs) + 1) * size, size)
        out_ref[at, :] = as_rows(in_ref, row_ref)


def halves_swapped(x):
    return jnp.concatenate([x[:, SPAN:], x[:, :SPAN]], axis=1)


def pair(low, first, second):
    even = jnp.where(low, first, halves_swapped(second))
    odd = jnp.where(low, halves_swapped(first), second)
    return even, odd


def low_lanes():
    return lax.broadcasted_iota(jnp.int32, (ROWS_OF_TILE, LANES), 1) < SPAN


def pair_kernel(tile_ref, out_ref):
    low = low_lanes()
    to = lax.broadcasted_iota(jnp.int32, (SPAN, SPAN), 0)
    row = lax.broadcasted_iota(jnp.int32, (SPAN, SPAN), 1)
    order = (row == to % 2 * ROWS_OF_TILE + to // 2).astype(jnp.bfloat16)
    for q in range(out_ref.shape[0] // SPAN):
        sides = []
        for t in range(0, PER_PART, 2):
            k = q * PER_PART + t
            halves = pair(
                low, *[tile_ref[pl.ds((k + i) * ROWS_OF_TILE, ROWS_OF_TILE), :] for i in (0, 1)]
            )
            sides.append(jnp.concatenate(halves, axis=0))
        both = jnp.concatenate(sides, axis=1)
        ordered = jnp.dot(order, both, preferred_element_type=jnp.float32)
        out_ref[pl.ds(q * SPAN, SPAN), :] = ordered.astype(jnp.bfloat16)


def partial_kernel(cd_ref, tile_ref, *refs):
    in_refs, (first_ref, second_ref, amp_ref) = refs[:-3], refs[-3:]
    low = low_lanes()
    me = lax.axis_index("outer")
    size = in_refs[0].shape[0]
    for by, in_ref in enumerate(reversed(in_refs)):
        amp_ref[tile_rows(source(by, me, len(in_refs)) * size, size), :] = in_ref[...]
    half = first_ref.shape[0] // ROWS_OF_TILE
    for q in range(2 * half):
        amps = []
        for t in range(0, PER_PART, 2):
            k = q * PER_PART + t
            amps.append(
                pair(low, *[amp_ref[tile_rows(cd_ref[k + i, 0]), :] for i in (0, 1)])
            )
        left = jnp.concatenate([jnp.concatenate([a[h] for a in amps], axis=1) for h in (0, 1)], axis=0)
        value = lax.dot_general(
            left,
            tile_ref[pl.ds(q * SPAN, SPAN), :],
            (((1,), (1,)), ((), ())),
            preferred_element_type=jnp.float32,
        )
        packed = jnp.concatenate([value[:ROWS_OF_TILE], value[ROWS_OF_TILE:]], axis=1)
        out_ref = first_ref if q < half else second_ref
        out_ref[pl.ds(q % half * ROWS_OF_TILE, ROWS_OF_TILE), :] = packed.astype(jnp.bfloat16)


def add_tiles(slot_ref, ref, sum_ref, start=0):
    for q in range(ref.shape[0] // ROWS_OF_TILE):
        at = tile_rows(slot_ref[start + q, 0])
        sum_ref[at, :] += ref[pl.ds(q * ROWS_OF_TILE, ROWS_OF_TILE), :].astype(jnp.float32)


def own_kernel(slot_ref, first_ref, second_ref, sum_ref):
    sum_ref[...] = jnp.zeros_like(sum_ref)
    add_tiles(slot_ref, first_ref, sum_ref)
    add_tiles(slot_ref, second_ref, sum_ref, first_ref.shape[0] // ROWS_OF_TILE)


def half_kernel(slot_ref, ref, in_ref, sum_ref):
    add_tiles(slot_ref, ref, sum_ref)


def other_kernel(slot_ref, ref, in_ref, *refs):
    out_refs, sum_ref = refs[:-1], refs[-1]
    add_tiles(slot_ref, ref, sum_ref, ref.shape[0] // ROWS_OF_TILE)
    for block, out_ref in enumerate(out_refs):
        size = out_ref.shape[0]
        out_ref[...] = sum_ref[pl.ds((block + 1) * size, size), :].astype(jnp.bfloat16)


def plane_kernel(others, own_ref, *refs):
    in_refs, out_refs = refs[:others], refs[others:]
    start = 0
    for out_ref in out_refs:
        at = pl.ds(start, out_ref.shape[0])
        total = own_ref[at, :]
        for ref in in_refs:
            total += ref[at, :].astype(jnp.float32)
        out_ref[...] = total.astype(out_ref.dtype)
        start += out_ref.shape[0]


def final_kernel(*refs):
    in_refs, (residual_ref, out_ref, sum_ref) = refs[:-3], refs[-3:]
    size = sum_ref.shape[0]
    blocks = [
        ref[pl.ds(first, size), :] for ref in in_refs for first in range(0, ref.shape[0], size)
    ]
    total = blocks[0].astype(jnp.float32)
    for block in blocks[1:]:
        total += block.astype(jnp.float32)
    sum_ref[...] = total
    tiles = size // ROWS_OF_TILE
    for i in range(ROWS_OF_TILE):
        at = pl.ds(i * LANES, LANES)
        out_ref[0, :, at] = residual_ref[0, :, at] + sum_ref[pl.ds(i, tiles, stride=ROWS_OF_TILE), :]


def permutes(sizes):
    places = list(itertools.product(*map(range, sizes)))
    number = {place: i for i, place in enumerate(places)}

    def moved(place, by):
        return tuple(
            a ^ b if n & (n - 1) == 0 else (a + b) % n for a, b, n in zip(place, by, sizes)
        )

    return {by: [(number[p], number[moved(p, by)]) for p in places] for by in places[1:]}


def exchange(blocks, axes, sizes):
    return [lax.ppermute(x, axes, pairs) for x, pairs in zip(blocks, permutes(sizes).values())][::-1]


def exchange_crossed(blocks, sizes, outer_core):
    outer, inner, groups, cores = sizes
    in_plane = [(0, *by, 0) for by in itertools.product(range(inner), range(groups))]
    pairs = permutes(sizes)
    line, total = inner * groups * cores, math.prod(sizes)
    arrived = []
    for i, x in enumerate(blocks, 1):
        across = pairs[in_plane[i if outer_core == 0 else (0, 2, 1, 3)[i]]]
        both = [
            (n, (n - i * line) % total) if n % cores == outer_core else across[n] for n in range(total)
        ]
        arrived.append(lax.ppermute(x, ("outer", "inner", "groups", "core"), both))
    return arrived[::-1]


def per_device(outer, inner, groups, cores, tiles, cd_tile, part_dest, place, amplitudes, residual_in):
    held, parts = tiles.shape[0], place.shape[0]
    own_cd = amplitudes.shape[1]
    per_col = residual_in.shape[1]
    bf16, f32 = jnp.bfloat16, jnp.float32
    shape = jax.ShapeDtypeStruct
    rows = outer * inner
    plane = inner * groups
    slots = rows * groups * per_col
    by_permutes = outer <= MOST_PERMUTED
    opposite = by_permutes and cores == 2 and outer == plane
    swap = [(i, (i + 1) % cores) for i in range(cores)]

    others = exchange([amplitudes] * (inner - 1), ("inner",), (inner,))[::-1]
    shard_rows = own_cd * ROWS_OF_TILE
    row_scratch = [pltpu.VMEM((shard_rows, LANES), f32)]
    sizes = outer, inner, groups, cores
    rows_of = lambda count: shape((count, LANES), jnp.int32)
    arguments = [
        amplitudes,
        cd_tile.reshape(1, held),
        part_dest.reshape(1, parts),
        place.reshape(1, parts),
    ]
    own, first_cd, own_slot, other_slot = call(
        functools.partial(layout_kernel, sizes, per_col, by_permutes, opposite),
        [shape((shard_rows, LANES), bf16), rows_of(held), rows_of(parts), rows_of(parts)],
        [pl.BlockSpec(memory_space=pltpu.HBM)] * len(arguments),
        *[pltpu.with_memory_space_constraint(x, pltpu.HBM) for x in arguments],
        scratch=row_scratch
        + [pltpu.VMEM(x.shape, x.dtype) for x in arguments]
        + [pltpu.SemaphoreType.DMA((len(arguments),))],
    )
    near = call(
        near_kernel,
        shape((inner * shard_rows, LANES), bf16),
        [VMEM] * inner,
        own,
        *others,
        scratch=row_scratch,
    )
    if by_permutes:
        gathered = exchange([near] * (outer - 1), ("outer",), (outer,))[::-1]
    else:
        repeated = jnp.broadcast_to(near, (outer,) + near.shape)
        gathered = lax.all_to_all(repeated, "outer", split_axis=0, concat_axis=0, tiled=True)
        gathered = [gathered.reshape(rows * shard_rows, LANES)]

    paired = call(
        pair_kernel,
        shape((parts * SPAN, PER_PART * SPAN), bf16),
        [VMEM],
        tiles.reshape(held * ROWS_OF_TILE, LANES),
    )
    if cores > 1:
        other_slot = lax.ppermute(other_slot, "core", swap)
    else:
        other_slot = jnp.full_like(other_slot, slots * ROWS_OF_TILE)
    gathered, paired, own_slot, other_slot, first_cd = lax.optimization_barrier(
        (gathered, paired, own_slot, other_slot, first_cd)
    )

    sources = gathered[::-1] + [near] if by_permutes else gathered
    partial = call(
        partial_kernel,
        [shape((parts // 2 * ROWS_OF_TILE, LANES), bf16)] * 2,
        [VMEM] * (2 + len(sources)),
        first_cd,
        paired,
        *sources,
        scratch=[pltpu.VMEM((rows * shard_rows, LANES), bf16)],
    )
    other = [lax.ppermute(x, "core", swap) for x in partial]
    summed = shape(((slots + 1) * ROWS_OF_TILE, LANES), f32)
    own_sum = call(own_kernel, summed, [VMEM] * 3, own_slot, *partial)
    own_sum = call(half_kernel, summed, [VMEM] * 3, other_slot, other[0], own_sum, aliases={2: 0})
    block = slots // plane * ROWS_OF_TILE
    *leaving, own_sum = call(
        other_kernel,
        [shape((block, LANES), bf16)] * (plane - 1) + [summed],
        [VMEM, VMEM, VMEM],
        other_slot,
        other[1],
        own_sum,
        aliases={2: plane - 1},
    )
    if opposite:
        arrived = exchange_crossed(leaving, sizes, 1)
    else:
        arrived = exchange(leaving, ("inner", "groups"), (inner, groups))
    mine = per_col * ROWS_OF_TILE
    if by_permutes:
        split = [shape((mine, LANES), f32)] + [shape((mine, LANES), bf16)] * (outer - 1)
    else:
        split = [shape((outer * mine, LANES), bf16)]
    sums = call(
        functools.partial(plane_kernel, len(arrived)),
        split,
        [VMEM] * (1 + len(arrived)),
        own_sum,
        *arrived,
    )
    if opposite:
        incoming = exchange_crossed(sums[1:], sizes, 0) + [sums[0]]
    elif by_permutes:
        incoming = exchange(sums[1:], ("outer",), (outer,)) + [sums[0]]
    else:
        incoming = [
            lax.all_to_all(
                sums[0].reshape(outer, mine, LANES), "outer", split_axis=0, concat_axis=0, tiled=True
            ).reshape(outer * mine, LANES)
        ]
    return call(
        final_kernel,
        shape(residual_in.shape, f32),
        [VMEM] * (len(incoming) + 1),
        *incoming,
        residual_in,
        scratch=[pltpu.VMEM((mine, LANES), f32)],
    )


def solution(mesh):
    rows, cols = mesh.shape["rows"], mesh.shape["cols"]
    inner = 2 if rows % 2 == 0 else 1
    cores = 2 if cols % 2 == 0 else 1
    axes = ("outer", "inner", "groups", "core")
    sizes = (rows // inner, inner, cols // cores, cores)
    split = Mesh(mesh.devices.reshape(sizes), axes)
    return jax.shard_map(
        functools.partial(per_device, *sizes),
        mesh=split,
        in_specs=(
            P(axes, None),
            P(axes),
            P(axes, None),
            P(axes),
            P(axes[2:], axes[:2], None),
            P(axes[:2], axes[2:], None),
        ),
        out_specs=P(axes[:2], axes[2:], None),
        check_vma=False,
    )
```
